32 devices in a mesh: wave: 4 (over x, core), deg: 8 (over z, y).
Axes of the slice: x: 2, y: 2, z: 4, core: 2. Of those that a mesh axis runs over, the one named last changes fastest.
Arguments:
- spectrum: bfloat16 [256, 2, 32, 2048], P('wave', None, None, 'deg'), may hold values from -2 to 2
- leaf_map: bfloat16 [256, 2048, 128], P('wave', 'deg'), may hold values from -0.375 to 0.375
- level_maps: bfloat16 [3, 256, 1024, 128], P(None, 'wave', 'deg'), may hold values from -0.5 to 0.5
- lat_map: bfloat16 [256, 128, 1024], P('wave', None, 'deg'), may hold values from -0.03125 to 0.03125
- skeleton: int32 [256, 1024], P('wave', 'deg'), may hold values from 0 to 255
- wavemap: int32 [256], replicated, may hold values from 0 to 4095, as said below
Outputs:
- grid: bfloat16 [32, 1024, 8192], P('wave', 'deg')
The draws below stay inside these ranges and needn't reach their ends.
Inputs may be any that keep to these rules, and one draw needn't show every extreme that they name: `skeleton`: for slot m and block b, entries b * 128 to b * 128 + 127 are degrees counted from the first degree of block b. `wavemap`: no two slots hold the same wavenumber.
All inputs are finite; a program needn't handle non-finite values.
Results may differ from the reference program's by a relative error of at most 0.0086.
Values may be sent and summed in bfloat16 or wider, within the bound.
No kernel may reach another device: no remote copies, remote signals or barrier semaphores. Data moves between devices by JAX's collectives and lax.ppermute only.
A program may use at most 192 MiB of HBM per device.

```python
import jax
import jax.numpy as jnp
from jax import lax

FL = 32
NODE = 128
NB = 256
WAVE_DEV = 64
WAVES = 256
LEVELS = 3
NLON = 8192
LONG_SPLIT = 32
DEGS = 2048
NLAT = 1024
N_WAVE = 4
N_DEG = 8


def draw_wavemap(key, part):
    half = NLON // 2
    inner = jax.random.permutation(jax.random.fold_in(key, 17), half - 2) + 1
    chosen = jnp.concatenate([jnp.array([0, half - 1], jnp.int32), inner[:WAVES - 2].astype(jnp.int32)])
    ordered = jnp.sort(chosen)
    rank_idx = jnp.arange(WAVES, dtype=jnp.int32)
    phase = rank_idx % (2 * N_WAVE)
    group = jnp.where(phase < N_WAVE, phase, 2 * N_WAVE - 1 - phase)
    slot = group * WAVE_DEV + rank_idx // N_WAVE
    return jnp.zeros((WAVES,), jnp.int32).at[slot].set(ordered)


def place_ends(values, stream_key, least, largest):
    longest = values.shape.index(max(values.shape))
    spots = []
    for shift in (0, 1):
        where = [jax.random.randint(jax.random.fold_in(stream_key, axis), (), 0, length) for axis, length in enumerate(values.shape)]
        where[longest] = (where[longest] + shift) % values.shape[longest]
        spots.append(tuple(where))
    return values.at[spots[0]].set(least).at[spots[1]].set(largest)


def levels(key, extent, shards, smallest, high):
    gain, own = 1.0, jax.random.fold_in(key, 6)
    for axis_at, parts in shards:
        heights = jnp.exp(jax.random.uniform(jax.random.fold_in(own, axis_at), (parts,), jnp.float32, smallest / len(shards), high / len(shards)))
        gain = gain * jnp.repeat(heights, extent[axis_at] // parts).reshape([-1 if axis == axis_at else 1 for axis in range(len(extent))])
    return gain


def bell_draw(rng, shape, width, bound, cuts=(), kind=jnp.bfloat16):
    entries = jax.random.normal(rng, shape, jnp.float32) * width
    if len(cuts) > 0:
        entries = levels(rng, shape, cuts, -0.22, 0.18) * entries
    return jnp.clip(entries, min=-bound, max=bound).astype(kind)


def setup_inputs(seed: int = 0) -> dict:
    splits = jax.random.split(jax.random.key(seed), 7)
    return {
        "spectrum": bell_draw(splits[0], (WAVES, 2, FL, DEGS), 0.35, 2.0, ((0, 4), (3, 8))),
        "leaf_map": bell_draw(splits[1], (WAVES, DEGS, NODE), NB ** -0.5, 0.375, ((0, 4), (1, 8))),
        "level_maps": bell_draw(splits[2], (LEVELS, WAVES, N_DEG * NODE, NODE), NODE ** -0.5, 0.5, ((1, 4), (2, 8))),
        "lat_map": bell_draw(splits[3], (WAVES, NODE, NLAT), (NODE * WAVES) ** -0.5, 0.03125, ((0, 4), (2, 8))),
        "skeleton": place_ends(jax.random.randint(splits[4], (WAVES, N_DEG * NODE), 0, NB), jax.random.fold_in(splits[4], 1), 0, NB - 1).astype(jnp.int32),
        "wavemap": draw_wavemap(jax.random.fold_in(splits[6], 71), 0),
    }


def long_tables(lon_count, first):
    half = lon_count // 2
    second = half // first
    a_idx = lax.broadcasted_iota(jnp.int32, (first, 2 * first), 0)
    u_idx = lax.broadcasted_iota(jnp.int32, (first, 2 * first), 1)
    ang1 = ((a_idx * u_idx) % (2 * first)).astype(jnp.float32) * (2.0 * jnp.pi / (2 * first))
    cos1 = jnp.cos(ang1)
    sin1 = jnp.sin(ang1)
    table1 = jnp.stack([jnp.stack([cos1, sin1], 1), jnp.stack([-sin1, cos1], 1)], 0).astype(jnp.bfloat16)
    e_idx = lax.broadcasted_iota(jnp.int32, (second, 2 * first), 0)
    w_idx = lax.broadcasted_iota(jnp.int32, (second, 2 * first), 1)
    ang_tw = ((e_idx * w_idx) % lon_count).astype(jnp.float32) * (2.0 * jnp.pi / lon_count)
    tw_cos = jnp.cos(ang_tw)
    tw_sin = jnp.sin(ang_tw)
    e2_idx = lax.broadcasted_iota(jnp.int32, (second, second), 0)
    v_idx = lax.broadcasted_iota(jnp.int32, (second, second), 1)
    ang2 = ((e2_idx * v_idx) % second).astype(jnp.float32) * (2.0 * jnp.pi / second)
    table2 = jnp.stack([jnp.cos(ang2), -jnp.sin(ang2)]).astype(jnp.bfloat16)
    return table1, tw_cos, tw_sin, table2


def long_synthesis(block, wavemap, lon_count, first):
    table1, tw_cos, tw_sin, table2 = long_tables(lon_count, first)
    half = lon_count // 2
    second = half // first
    field_count = block.shape[2]
    row_count = block.shape[3]
    weight = jnp.where(wavemap == 0, 1.0, 2.0).astype(jnp.float32)[:, None, None, None]
    scaled = (weight * block.astype(jnp.float32)).astype(jnp.bfloat16)
    coeffs = jnp.zeros((half, 2, field_count, row_count), jnp.bfloat16).at[wavemap.astype(jnp.int32)].set(scaled)
    coeffs = coeffs.reshape(first, second, 2, field_count, row_count)
    section = jnp.einsum("aerfl,rapu->epufl", coeffs.astype(jnp.float32), table1.astype(jnp.float32))
    real_part = section[:, 0]
    imag_part = section[:, 1]
    tc = tw_cos[:, :, None, None]
    ts = tw_sin[:, :, None, None]
    twisted = jnp.stack([real_part * tc - imag_part * ts, real_part * ts + imag_part * tc], 1).astype(jnp.bfloat16)
    result = jnp.einsum("epufl,pev->flvu", twisted.astype(jnp.float32), table2.astype(jnp.float32))
    return result.reshape(field_count, row_count, lon_count).astype(jnp.bfloat16)


def one_slot(spec_slot, leaf_slot, levels_slot, lat_slot, skel_slot):
    field_count = spec_slot.shape[1]
    columns = 2 * field_count
    flat_coef = spec_slot.reshape(columns, N_DEG, -1).transpose(1, 0, 2)
    node_width = leaf_slot.shape[1]
    half_width = node_width // 2
    skel_index = jnp.broadcast_to(skel_slot.reshape(N_DEG, 1, node_width), (N_DEG, columns, node_width))
    picked = jnp.take_along_axis(flat_coef, skel_index, axis=2)
    leaf_rows = leaf_slot.reshape(N_DEG, -1, node_width)
    node_state = (picked.astype(jnp.float32) + jnp.einsum("bcn,bnk->bck", flat_coef.astype(jnp.float32), leaf_rows.astype(jnp.float32))).astype(jnp.bfloat16)
    blocks = jnp.arange(N_DEG, dtype=jnp.int32)
    for level_num in range(LEVELS):
        low_block = blocks - (blocks & (1 << level_num))
        high_block = low_block + (1 << level_num)
        upper_bit = ((blocks >> level_num) & 1)[:, None, None]
        low_side = node_state[low_block]
        high_side = node_state[high_block]
        low_half = jnp.where(upper_bit == 0, low_side[:, :, :half_width], low_side[:, :, half_width:])
        high_half = jnp.where(upper_bit == 0, high_side[:, :, :half_width], high_side[:, :, half_width:])
        joined = jnp.concatenate([low_half, high_half], axis=2)
        factor = levels_slot[level_num].reshape(N_DEG, node_width, node_width)
        node_state = jnp.einsum("bck,bks->bcs", joined.astype(jnp.float32), factor.astype(jnp.float32)).astype(jnp.bfloat16)
    lat_rows = lat_slot.reshape(node_width, N_DEG, -1)
    lat_values = jnp.einsum("bck,kbl->cbl", node_state.astype(jnp.float32), lat_rows.astype(jnp.float32)).astype(jnp.bfloat16)
    return lat_values.reshape(columns, -1)


def reference(spectrum, leaf_map, level_maps, lat_map, skeleton, wavemap):
    slot_total = spectrum.shape[0]
    field_count = spectrum.shape[2]

    def per_slot(slot):
        return one_slot(spectrum[slot], leaf_map[slot], level_maps[:, slot], lat_map[slot], skeleton[slot])

    lat_values = lax.map(per_slot, jnp.arange(slot_total, dtype=jnp.int32))
    split_values = lat_values.reshape(slot_total, 2, field_count, -1)

    def per_field(field_num):
        chosen = lax.dynamic_slice_in_dim(split_values, field_num, 1, 2)
        return long_synthesis(chosen, wavemap, NLON, LONG_SPLIT)[0]

    return lax.map(per_field, jnp.arange(field_count, dtype=jnp.int32))
```

```python
import jax
import jax.numpy as jnp
from jax import lax
from jax.sharding import PartitionSpec as P

NLON = 8192


def partner(shard, axis, bit):
    return lax.ppermute(shard, axis, [(i, i ^ 1 << bit) for i in range(lax.axis_size(axis))])


def wave_table(wavemap, lon_count):
    lanes = 128
    slots = wavemap.shape[0]
    scale = 2.0 * jnp.pi / lon_count
    q = wavemap[:, None]
    low = lax.broadcasted_iota(jnp.int32, (slots, lanes), 1)
    high = lanes * lax.broadcasted_iota(jnp.int32, (slots, lon_count // lanes), 1)
    low_angle = (q * low % lon_count).astype(jnp.float32) * scale
    high_angle = (q * high % lon_count).astype(jnp.float32) * scale
    weight = jnp.where(q == 0, 1.0, 2.0).astype(jnp.float32)
    cos_low, sin_low = (jnp.cos(low_angle) * weight)[:, None, :], (jnp.sin(low_angle) * weight)[:, None, :]
    cos_high, sin_high = jnp.cos(high_angle)[:, :, None], jnp.sin(high_angle)[:, :, None]
    cos_all = (cos_high * cos_low - sin_high * sin_low).reshape(slots, lon_count)
    sin_all = (sin_high * cos_low + cos_high * sin_low).reshape(slots, lon_count)
    return jnp.stack([cos_all, -sin_all]).astype(jnp.bfloat16)


def body(spectrum, leaf_map, level_maps, lat_map, skeleton, wavemap):
    slot_count = spectrum.shape[0]
    field_count = spectrum.shape[2]
    columns = 2 * field_count
    node_width = leaf_map.shape[2]
    half_width = node_width // 2
    flat_coef = spectrum.reshape(slot_count, columns, -1)
    degree_count = flat_coef.shape[2]
    degree_iota = lax.broadcasted_iota(jnp.int32, (slot_count, degree_count, node_width), 1)
    selector = (degree_iota == skeleton[:, None, :]).astype(jnp.bfloat16)
    picked = jnp.einsum("mcn,mnk->mck", flat_coef, selector, preferred_element_type=jnp.float32)
    node_state = (
        picked + jnp.einsum("mcn,mnk->mck", flat_coef, leaf_map, preferred_element_type=jnp.float32)
    ).astype(jnp.bfloat16)
    deg_index = lax.axis_index("deg")
    for level_num in range(level_maps.shape[0]):
        upper_bit = deg_index >> level_num & 1
        own_half = lax.dynamic_slice_in_dim(node_state, upper_bit * half_width, half_width, 2)
        payload = lax.dynamic_slice_in_dim(node_state, (1 - upper_bit) * half_width, half_width, 2)
        packed = payload.reshape(slot_count, columns // 2, 2 * half_width)
        factor = level_maps[level_num]
        own_rows = lax.dynamic_slice_in_dim(factor, upper_bit * half_width, half_width, 1)
        other_rows = lax.dynamic_slice_in_dim(factor, (1 - upper_bit) * half_width, half_width, 1)
        own_term = jnp.einsum(
            "mck,mks->mcs", own_half, own_rows, preferred_element_type=jnp.float32
        )
        arrived = partner(packed, "deg", level_num).reshape(payload.shape)
        other_term = jnp.einsum(
            "mck,mks->mcs", arrived, other_rows, preferred_element_type=jnp.float32
        )
        node_state = (own_term + other_term).astype(jnp.bfloat16)
    lat_values = jnp.einsum(
        "mck,mkl->mcl", node_state, lat_map, preferred_element_type=jnp.float32
    ).astype(jnp.bfloat16)
    lat_values = lat_values.reshape(slot_count, 2, field_count, -1)
    gathered = lax.all_to_all(lat_values, "wave", split_axis=2, concat_axis=0, tiled=True)
    local_fields = gathered.shape[2]
    row_count = gathered.shape[3]
    table = wave_table(wavemap, NLON)
    result = jnp.einsum("mrfl,rmn->fln", gathered, table, preferred_element_type=jnp.float32)
    return result.astype(jnp.bfloat16)


def solution(mesh):
    placed = (
        P("wave", None, None, "deg"),
        P("wave", "deg", None),
        P(None, "wave", "deg", None),
        P("wave", None, "deg"),
        P("wave", "deg"),
        P(),
    )
    return jax.shard_map(
        body, mesh=mesh, in_specs=placed, out_specs=P("wave", "deg", None), check_vma=False
    )
```

```python
import functools

import jax
import jax.numpy as jnp
from jax import lax
from jax.experimental import pallas as pl
from jax.experimental.pallas import tpu as pltpu
from jax.sharding import PartitionSpec as P

NLON = 8192
CHUNKS = 2
GROUP = 16
LANES = 128
VMEM = 48 * 2**20


def exchange(shard, axis, step):
    return lax.ppermute(shard, axis, [(i, i ^ step) for i in range(lax.axis_size(axis))])


def low_lanes(rows, width):
    return lax.broadcasted_iota(jnp.int32, (rows, width), 1) < width // 2


def split_halves(state):
    fields, width = state.shape[0] // 2, state.shape[1]
    real, imag = state[:fields], state[fields:]
    low = low_lanes(fields, width)
    first = jnp.where(low, real, pltpu.roll(imag, width // 2, 1))
    second = jnp.where(low, pltpu.roll(real, width // 2, 1), imag)
    return first.astype(jnp.bfloat16), second.astype(jnp.bfloat16)


def join_halves(first, second):
    fields, width = first.shape
    low = low_lanes(fields, width)
    first, second = first.astype(jnp.float32), second.astype(jnp.float32)
    real = jnp.where(low, first, pltpu.roll(second, width // 2, 1))
    imag = jnp.where(low, pltpu.roll(first, width // 2, 1), second)
    return jnp.concatenate([real, imag], 0).astype(jnp.bfloat16)


def dot(a, b):
    return jnp.dot(a, b, preferred_element_type=jnp.float32)


def put_halves(upper, state, own_ref, send_ref, g):
    first, second = split_halves(state)
    own_ref[g] = jnp.where(upper == 1, second, first)
    send_ref[g] = jnp.where(upper == 1, first, second)


def joined_state(upper, own_ref, came_ref, g):
    own, came = own_ref[g], came_ref[g]
    return join_halves(jnp.where(upper == 1, came, own), jnp.where(upper == 1, own, came))


def leaf_kernel(upper_ref, coef_ref, map_ref, skel_ref, own_ref, send_ref):
    degrees, width = map_ref.shape[1:]
    rows = lax.broadcasted_iota(jnp.int32, (degrees, width), 0)
    for g in range(coef_ref.shape[0]):
        picks = (rows == skel_ref[g : g + 1, :]).astype(jnp.bfloat16)
        both = dot(coef_ref[g], jnp.concatenate([map_ref[g], picks], 1))
        put_halves(upper_ref[0], both[:, :width] + both[:, width:], own_ref, send_ref, g)


def level_kernel(upper_ref, own_in, came_in, map_ref, own_ref, send_ref):
    for g in range(own_in.shape[0]):
        joined = joined_state(upper_ref[0], own_in, came_in, g)
        put_halves(upper_ref[1], dot(joined, map_ref[0, g]), own_ref, send_ref, g)


def last_kernel(upper_ref, own_in, came_in, map_ref, lat_ref, *refs):
    out_refs, block_ref = refs[:-1], refs[-1]
    group, fields = own_in.shape[:2]
    peers = len(out_refs)
    share = fields // peers
    for g in range(group):
        joined = joined_state(upper_ref[0], own_in, came_in, g)
        node = dot(joined, map_ref[0, g]).astype(jnp.bfloat16)
        block_ref[g] = dot(node, lat_ref[g]).astype(jnp.bfloat16)
    tile = 16
    size = group * tile
    out_at = lax.broadcasted_iota(jnp.int32, (size, size), 0)
    in_at = lax.broadcasted_iota(jnp.int32, (size, size), 1)
    swap = ((out_at // group == in_at % tile) & (out_at % group == in_at // tile)).astype(jnp.bfloat16)
    rows = block_ref.shape[2]
    for c in range(0, 2 * fields, tile):
        moved = dot(swap, block_ref[:, c : c + tile, :].reshape(size, rows)).astype(jnp.bfloat16)
        moved = moved.reshape(tile, group, rows)
        part, first = c // fields, c % fields
        for at in range(0, tile, share):
            peer = (first + at) // share
            for step in range(peers):

                @pl.when((upper_ref[1] ^ peer) == step)
                def _():
                    out_refs[step][:, part, :, :] = moved[at : at + share]


def table_kernel(cos_low, sin_low, cos_high, sin_high, table_ref):
    cl, sl = cos_low[...], sin_low[...]
    for h in range(cos_high.shape[1]):
        ch, sh = cos_high[:, h : h + 1], sin_high[:, h : h + 1]
        table_ref[0, 0, :, h * LANES : (h + 1) * LANES] = (ch * cl - sh * sl).astype(jnp.bfloat16)
        table_ref[0, 1, :, h * LANES : (h + 1) * LANES] = (-(sh * cl) - ch * sl).astype(jnp.bfloat16)


def wave_table(slots, lon_count):
    blocks, count = slots.shape
    high = lon_count // LANES
    scale = 2.0 * jnp.pi / lon_count
    q = slots.reshape(-1, 1)
    total = q.shape[0]
    low_at = lax.broadcasted_iota(jnp.int32, (total, LANES), 1)
    high_at = LANES * lax.broadcasted_iota(jnp.int32, (total, high), 1)
    low_angle = (q * low_at % lon_count).astype(jnp.float32) * scale
    high_angle = (q * high_at % lon_count).astype(jnp.float32) * scale
    weight = jnp.where(q == 0, 1.0, 2.0).astype(jnp.float32)
    low_spec = pl.BlockSpec((count, LANES), lambda i: (i, 0))
    high_spec = pl.BlockSpec((count, high), lambda i: (i, 0))
    return pl.pallas_call(
        table_kernel,
        grid=(blocks,),
        in_specs=[low_spec, low_spec, high_spec, high_spec],
        out_specs=pl.BlockSpec((1, 2, count, lon_count), lambda i: (i, 0, 0, 0)),
        out_shape=jax.ShapeDtypeStruct((blocks, 2, count, lon_count), jnp.bfloat16),
        cost_estimate=pl.CostEstimate(
            flops=8 * total * lon_count, bytes_accessed=4 * total * lon_count, transcendentals=0
        ),
        compiler_params=pltpu.CompilerParams(vmem_limit_bytes=VMEM),
        name="table",
    )(
        jnp.cos(low_angle) * weight,
        jnp.sin(low_angle) * weight,
        jnp.cos(high_angle),
        jnp.sin(high_angle),
    )


def synthesis_kernel(*refs):
    block_refs, table_ref, out_ref, left_ref = refs[:-3], refs[-3], refs[-2], refs[-1]
    fields, rows = out_ref.shape[:2]

    @pl.when(pl.program_id(0) == 0)
    def _():
        for f in range(fields):
            parts = [ref[f].reshape(-1, rows) for ref in block_refs]
            left_ref[f * rows : (f + 1) * rows, :] = jnp.concatenate(parts, 0).T

    out = dot(left_ref[...], table_ref[...]).astype(jnp.bfloat16)
    out_ref[...] = out.reshape(out_ref.shape)


def synthesis(blocks, table):
    fields, _, _, rows = blocks[0].shape
    depth, lon_count = table.shape
    width = 8 * LANES
    return pl.pallas_call(
        synthesis_kernel,
        grid=(lon_count // width,),
        in_specs=[pl.BlockSpec(b.shape, lambda i: (0, 0, 0, 0)) for b in blocks]
        + [pl.BlockSpec((depth, width), lambda i: (0, i))],
        out_specs=pl.BlockSpec((fields, rows, width), lambda i: (0, 0, i)),
        out_shape=jax.ShapeDtypeStruct((fields, rows, lon_count), jnp.bfloat16),
        scratch_shapes=[pltpu.VMEM((fields * rows, depth), jnp.bfloat16)],
        cost_estimate=pl.CostEstimate(
            flops=2 * fields * rows * depth * lon_count,
            bytes_accessed=2 * lon_count * (fields * rows + depth),
            transcendentals=0,
        ),
        compiler_params=pltpu.CompilerParams(vmem_limit_bytes=VMEM),
        name="synthesis",
    )(*blocks, table)


def slot_spec(shape, first=0, lead=None):
    if lead is None:
        return pl.BlockSpec((GROUP,) + shape[1:], lambda i: (first + i,) + (0,) * (len(shape) - 1))
    return pl.BlockSpec((1, GROUP) + shape[2:], lambda i: (lead, first + i) + (0,) * (len(shape) - 2))


def body(spectrum, leaf_map, level_maps, lat_map, skeleton, wavemap):
    slots, _, fields, degrees = spectrum.shape
    columns = 2 * fields
    width = leaf_map.shape[2]
    levels = level_maps.shape[0]
    rows = lat_map.shape[2]
    coef = spectrum.reshape(slots, columns, degrees)
    peers = lax.axis_size("wave")
    me = lax.axis_index("wave")
    place = lax.axis_index("deg")
    bits = [place >> level & 1 for level in range(levels)]
    count = slots // CHUNKS
    steps = count // GROUP
    scalar = pl.BlockSpec(memory_space=pltpu.SMEM)
    params = pltpu.CompilerParams(vmem_limit_bytes=VMEM)
    half = jax.ShapeDtypeStruct((count, fields, width), jnp.bfloat16)
    half_spec = slot_spec(half.shape)

    def leaf(chunk):
        first = chunk * steps
        return pl.pallas_call(
            leaf_kernel,
            grid=(steps,),
            in_specs=[
                scalar,
                slot_spec(coef.shape, first),
                slot_spec(leaf_map.shape, first),
                slot_spec(skeleton.shape, first),
            ],
            out_specs=[half_spec, half_spec],
            out_shape=[half, half],
            cost_estimate=pl.CostEstimate(
                flops=4 * count * columns * degrees * width,
                bytes_accessed=2 * count * degrees * (columns + width),
                transcendentals=0,
            ),
            compiler_params=params,
            name="leaf",
        )(jnp.stack(bits[:1]), coef, leaf_map, skeleton)

    def level(chunk, num, own, came):
        first = chunk * steps
        return pl.pallas_call(
            level_kernel,
            grid=(steps,),
            in_specs=[scalar, half_spec, half_spec, slot_spec(level_maps.shape, first, num)],
            out_specs=[half_spec, half_spec],
            out_shape=[half, half],
            cost_estimate=pl.CostEstimate(
                flops=2 * count * columns * width * width,
                bytes_accessed=2 * count * width * (width + 2 * columns),
                transcendentals=0,
            ),
            compiler_params=params,
            name="level",
        )(jnp.stack(bits[num : num + 2]), own, came, level_maps)

    def last(chunk, own, came):
        first = chunk * steps
        share = fields // peers
        piece = jax.ShapeDtypeStruct((share, 2, count, rows), jnp.bfloat16)
        return pl.pallas_call(
            last_kernel,
            grid=(steps,),
            in_specs=[
                scalar,
                half_spec,
                half_spec,
                slot_spec(level_maps.shape, first, levels - 1),
                slot_spec(lat_map.shape, first),
            ],
            out_specs=[pl.BlockSpec((share, 2, GROUP, rows), lambda i: (0, 0, i, 0))] * peers,
            out_shape=[piece] * peers,
            scratch_shapes=[pltpu.VMEM((GROUP, columns, rows), jnp.bfloat16)],
            cost_estimate=pl.CostEstimate(
                flops=2 * count * columns * width * (width + rows),
                bytes_accessed=2 * count * width * (width + rows + 2 * columns),
                transcendentals=0,
            ),
            compiler_params=params,
            name="last",
        )(jnp.stack([bits[-1], me]), own, came, level_maps, lat_map)

    state = [leaf(chunk) for chunk in range(CHUNKS)]
    for num in range(levels):
        for chunk in range(CHUNKS):
            own, send = state[chunk]
            came = exchange(send, "deg", 1 << num)
            if num + 1 < levels:
                state[chunk] = level(chunk, num, own, came)
            else:
                state[chunk] = last(chunk, own, came)
    blocks = []
    for chunk in range(CHUNKS):
        for step in range(peers):
            piece = state[chunk][step]
            blocks.append(piece if step == 0 else exchange(piece, "wave", step))

    by_peer = wavemap.reshape(peers, CHUNKS, count)
    order = by_peer[me ^ jnp.arange(peers)].transpose(1, 0, 2).reshape(CHUNKS * peers, count)
    table = wave_table(order, NLON).reshape(-1, NLON)
    return synthesis(blocks, table)


def solution(mesh):
    placed = (
        P("wave", None, None, "deg"),
        P("wave", "deg", None),
        P(None, "wave", "deg", None),
        P("wave", None, "deg"),
        P("wave", "deg"),
        P(),
    )
    return jax.shard_map(
        body, mesh=mesh, in_specs=placed, out_specs=P("wave", "deg", None), check_vma=False
    )
```

```python
import functools

import jax
import jax.numpy as jnp
from jax import lax
from jax.experimental import pallas as pl
from jax.experimental.pallas import tpu as pltpu
from jax.sharding import PartitionSpec as P

NLON = 8192
SHARES = (1, 1)
LANES = 128
PARTS = 4
TILE = 512
ROWS = 256
SLOTS = 3
IN_ANY = pl.BlockSpec(memory_space=pl.ANY)
IN_VMEM = pl.BlockSpec(memory_space=pltpu.VMEM)


def stay(array):
    return pltpu.with_memory_space_constraint(array, pltpu.HBM)


def exchange(shard, axis, step):
    return lax.ppermute(shard, axis, [(i, i ^ step) for i in range(lax.axis_size(axis))])


def low_lanes(rows, width):
    return lax.broadcasted_iota(jnp.int32, (rows, width), 1) < width // 2


def split_halves(state):
    fields, width = state.shape[0] // 2, state.shape[1]
    real, imag = state[:fields], state[fields:]
    low = low_lanes(fields, width)
    first = jnp.where(low, real, pltpu.roll(imag, width // 2, 1))
    second = jnp.where(low, pltpu.roll(real, width // 2, 1), imag)
    return first.astype(jnp.bfloat16), second.astype(jnp.bfloat16)


def join_halves(first, second):
    fields, width = first.shape
    low = low_lanes(fields, width)
    first, second = first.astype(jnp.float32), second.astype(jnp.float32)
    real = jnp.where(low, first, pltpu.roll(second, width // 2, 1))
    imag = jnp.where(low, pltpu.roll(first, width // 2, 1), second)
    return jnp.concatenate([real, imag], 0).astype(jnp.bfloat16)


def dot(a, b):
    return jnp.dot(a, b, preferred_element_type=jnp.float32)


def upper_bit(level):
    return lax.axis_index("deg") >> level & 1


def put_halves(upper, state, own_ref, send_ref, g):
    first, second = split_halves(state)
    own_ref[g] = jnp.where(upper == 1, second, first)
    send_ref[g] = jnp.where(upper == 1, first, second)


def joined_state(upper, own_ref, came_ref, g):
    own, came = own_ref[g], came_ref[g]
    return join_halves(jnp.where(upper == 1, came, own), jnp.where(upper == 1, own, came))


def load_parts(source, target, sems):
    part = target.shape[0] // PARTS
    copies = []
    for n in range(PARTS):
        here = pl.ds(n * part, part)
        copies.append(pltpu.make_async_copy(source.at[here], target.at[here], sems.at[n]))
        copies[-1].start()
    return copies


def start_fetches(places, sources, targets, sems):
    copies = []
    for n, (place, source, target) in enumerate(zip(places, sources, targets)):
        copies.append(pltpu.make_async_copy(source.at[place], target, sems.at[n]))
        copies[-1].start()
    return copies


def leaf_kernel(places, *refs):
    fetches = len(places)
    coef, maps, skel, _, *sources = refs[: 4 + fetches]
    own_ref, send_ref, *targets = refs[4 + fetches : 6 + 2 * fetches]
    count, _, width = own_ref.shape
    degrees = maps.shape[1]
    scratch = refs[6 + 2 * fetches :]
    parts = []
    if len(scratch) > 1:
        coef_hbm, map_hbm, skel_hbm = coef, maps, skel
        coef, maps, skel, sems = scratch[:4]
        skel_copy = pltpu.make_async_copy(skel_hbm.at[pl.ds(0, count)], skel, sems.at[2, 0])
        skel_copy.start()
        parts = [load_parts(map_hbm, maps, sems.at[0]), load_parts(coef_hbm, coef, sems.at[1])]
    later = start_fetches(places, sources, targets, scratch[-1])
    if parts:
        skel_copy.wait()
    rows = lax.broadcasted_iota(jnp.int32, (degrees, width), 0)
    for g in range(count):
        for copies in parts:
            if g % (count // PARTS) == 0:
                copies[g // (count // PARTS)].wait()
        picks = (rows == skel[g : g + 1, :]).astype(jnp.bfloat16)
        both = dot(coef[g], jnp.concatenate([maps[g], picks], 1))
        put_halves(upper_bit(0), both[:, :width] + both[:, width:], own_ref, send_ref, g)
    for copy in later:
        copy.wait()


def level_kernel(first, num, places, *refs):
    fetches = len(places)
    own_in, came_in, maps, _, *sources = refs[: 4 + fetches]
    own_ref, send_ref, *targets = refs[4 + fetches : 6 + 2 * fetches]
    later = start_fetches(places, sources, targets, refs[-1]) if fetches else []
    for g in range(own_in.shape[0]):
        joined = joined_state(upper_bit(num), own_in, came_in, g)
        put_halves(upper_bit(num + 1), dot(joined, maps[first + g]), own_ref, send_ref, g)
    for copy in later:
        copy.wait()


def last_kernel(first, num, own_in, came_in, maps, lats, _, *refs):
    out_refs, block_ref = refs[:-1], refs[-1]
    count, fields = own_in.shape[:2]
    peers = len(out_refs)
    share = fields // peers
    for g in range(count):
        joined = joined_state(upper_bit(num), own_in, came_in, g)
        node = dot(joined, maps[first + g]).astype(jnp.bfloat16)
        block_ref[g] = dot(node, lats[first + g]).astype(jnp.bfloat16)
    tile = 16
    size = tile * tile
    out_at = lax.broadcasted_iota(jnp.int32, (size, size), 0)
    in_at = lax.broadcasted_iota(jnp.int32, (size, size), 1)
    swap = ((out_at // tile == in_at % tile) & (out_at % tile == in_at // tile)).astype(jnp.bfloat16)
    rows = block_ref.shape[2]
    me = lax.axis_index("wave")
    for g in range(0, count, tile):
        for c in range(0, 2 * fields, tile):
            moved = dot(swap, block_ref[g : g + tile, c : c + tile, :].reshape(size, rows)).astype(jnp.bfloat16)
            moved = moved.reshape(tile, tile, rows)
            part, field = c // fields, c % fields
            for at in range(0, tile, share):
                peer = (field + at) // share
                for step in range(peers):

                    @pl.when((me ^ peer) == step)
                    def _():
                        out_refs[step][:, part, g : g + tile, :] = moved[at : at + share]


def table_kernel(lon_count, slots, sizes, map_ref, after_ref, table_ref, q_ref):
    me = lax.axis_index("wave")
    row = 0
    for n, size in enumerate(sizes):
        for step in range(map_ref.shape[0] // slots):
            start = (me ^ step) * slots + sum(sizes[:n])

            def put(m, carry, row=row, start=start):
                q_ref[pl.ds(row + m, 1), :] = jnp.full((1, LANES), map_ref[start + m], jnp.int32)
                return carry

            lax.fori_loop(0, size, put, 0, unroll=8)
            row += size
    scale = 2.0 * jnp.pi / lon_count
    lane = lax.broadcasted_iota(jnp.int32, (16, LANES), 1)

    def rows(i, carry):
        here = pl.ds(pl.multiple_of(i * 16, 16), 16)
        q = q_ref[here, :]
        low = (q * lane % lon_count).astype(jnp.float32) * scale
        high = (q * (lane * LANES) % lon_count).astype(jnp.float32) * scale
        weight = jnp.where(q == 0, 1.0, 2.0).astype(jnp.float32)
        cl, sl = jnp.cos(low) * weight, jnp.sin(low) * -weight
        ch, sh = jnp.cos(high), jnp.sin(high)
        for h in range(table_ref.shape[2] // LANES):
            c, s = ch[:, h : h + 1], sh[:, h : h + 1]
            table_ref[0, here, h * LANES : (h + 1) * LANES] = (c * cl + s * sl).astype(jnp.bfloat16)
            table_ref[1, here, h * LANES : (h + 1) * LANES] = (c * sl - s * cl).astype(jnp.bfloat16)
        return carry

    lax.fori_loop(0, q_ref.shape[0] // 16, rows, 0)


def wave_table(wavemap, slots, sizes, lon_count, after):
    total = wavemap.shape[0]
    return pl.pallas_call(
        functools.partial(table_kernel, lon_count, slots, sizes),
        in_specs=[pl.BlockSpec(memory_space=pltpu.SMEM), IN_ANY],
        out_specs=IN_VMEM,
        out_shape=jax.ShapeDtypeStruct((2, total, lon_count // 2 + LANES), jnp.bfloat16),
        scratch_shapes=[pltpu.VMEM((total, LANES), jnp.int32)],
        cost_estimate=pl.CostEstimate(
            flops=8 * total * lon_count, bytes_accessed=8 * total * lon_count, transcendentals=0
        ),
        compiler_params=pltpu.CompilerParams(vmem_limit_bytes=16 * 2**20),
        name="table",
    )(wavemap, after)


def synthesis_kernel(*refs):
    block_refs = refs[:-6]
    table_ref, out_ref, left_ref, carry_ref, buffer_ref, sems = refs[-6:]
    fields, rows, lon_count = out_ref.shape
    slots, width = buffer_ref.shape[0], buffer_ref.shape[-1]
    for f in range(fields):
        for p in range(2):
            left_ref[p, f * rows : (f + 1) * rows, :] = jnp.concatenate([ref[f, p] for ref in block_refs], 0).T
    middle = pl.ds(lon_count // 2, LANES)
    carry_ref[...] = dot(left_ref[0], table_ref[0, :, middle]) - dot(left_ref[1], table_ref[1, :, middle])
    tiles = lon_count // width
    steps = tiles // 2
    size = ROWS
    lane = lax.broadcasted_iota(jnp.int32, (size, LANES), 1)
    mirror = (LANES - lane) % LANES

    def copies(i):
        slot, at = i % slots, steps - 1 - i
        straight = pl.ds(pl.multiple_of(at * width, width), width)
        turned = pl.ds(pl.multiple_of((tiles - 1 - at) * width, width), width)
        return (
            pltpu.make_async_copy(buffer_ref.at[slot, 0], out_ref.at[:, :, straight], sems.at[slot, 0]),
            pltpu.make_async_copy(buffer_ref.at[slot, 1], out_ref.at[:, :, turned], sems.at[slot, 1]),
        )

    def step(i, carry):
        slot, at = i % slots, steps - 1 - i
        straight = pl.ds(pl.multiple_of(at * width, width), width)

        @pl.when(i >= slots)
        def _():
            for copy in copies(i - slots):
                copy.wait()

        for r in range(0, fields * rows, size):
            f = r // rows
            n = size // rows
            cos_sum = dot(left_ref[0, r : r + size, :], table_ref[0, :, straight])
            sin_sum = dot(left_ref[1, r : r + size, :], table_ref[1, :, straight])
            buffer_ref[slot, 0, f : f + n] = (cos_sum + sin_sum).astype(jnp.bfloat16).reshape(n, rows, width)
            back = cos_sum - sin_sum
            following = carry_ref[r : r + size, :]
            for t in reversed(range(width // LANES)):
                piece = back[:, t * LANES : (t + 1) * LANES]
                turned = jnp.take_along_axis(piece, mirror, axis=1, mode="promise_in_bounds")
                turned = jnp.where(lane == 0, following, turned).astype(jnp.bfloat16)
                to = width - (t + 1) * LANES
                buffer_ref[slot, 1, f : f + n, :, to : to + LANES] = turned.reshape(n, rows, LANES)
                following = piece
            carry_ref[r : r + size, :] = following
        for copy in copies(i):
            copy.start()
        return carry

    lax.fori_loop(0, steps, step, 0)
    for i in range(max(0, steps - slots), steps):
        for copy in copies(i):
            copy.wait()


def synthesis(blocks, table, lon_count):
    fields, _, _, rows = blocks[0].shape
    depth = table.shape[1]
    return pl.pallas_call(
        synthesis_kernel,
        in_specs=[IN_VMEM] * (len(blocks) + 1),
        out_specs=pl.BlockSpec(memory_space=pl.ANY),
        out_shape=jax.ShapeDtypeStruct((fields, rows, lon_count), jnp.bfloat16),
        scratch_shapes=[
            pltpu.VMEM((2, fields * rows, depth), jnp.bfloat16),
            pltpu.VMEM((fields * rows, LANES), jnp.float32),
            pltpu.VMEM((SLOTS, 2, fields, rows, TILE), jnp.bfloat16),
            pltpu.SemaphoreType.DMA((SLOTS, 2)),
        ],
        cost_estimate=pl.CostEstimate(
            flops=2 * fields * rows * depth * lon_count,
            bytes_accessed=2 * lon_count * (fields * rows + depth),
            transcendentals=0,
        ),
        compiler_params=pltpu.CompilerParams(vmem_limit_bytes=32 * 2**20),
        name="synthesis",
    )(*blocks, table)


def body(spectrum, leaf_map, level_maps, lat_map, skeleton, wavemap):
    slots, _, fields, degrees = spectrum.shape
    columns = 2 * fields
    width = leaf_map.shape[2]
    levels = level_maps.shape[0]
    rows = lat_map.shape[2]
    coef = spectrum.reshape(slots, columns, degrees)
    peers = lax.axis_size("wave")
    sizes = [slots * share // sum(SHARES) for share in SHARES]
    firsts = [sum(sizes[:n]) for n in range(len(sizes))]
    chunks = range(len(sizes))
    params = pltpu.CompilerParams(vmem_limit_bytes=16 * 2**20)

    def half(chunk):
        return jax.ShapeDtypeStruct((sizes[chunk], fields, width), jnp.bfloat16)

    def fetched(fetches):
        shapes = []
        for array, place in fetches:
            view = jax.eval_shape(lambda a, place=place: a[place], array)
            shapes.append(jax.ShapeDtypeStruct(view.shape, view.dtype))
        sems = [pltpu.SemaphoreType.DMA((len(fetches),))] if fetches else []
        return [stay(array) for array, _ in fetches], [at(place) for _, place in fetches], shapes, sems

    def at(place):
        return pl.ds(place.start, place.stop - place.start) if isinstance(place, slice) else place

    def leaf(chunk, inputs, after, fetches):
        count = sizes[chunk]
        sources, places, shapes, sems = fetched(fetches)
        scratch = [] if chunk else [
            pltpu.VMEM((count, columns, degrees), jnp.bfloat16),
            pltpu.VMEM((count, degrees, width), jnp.bfloat16),
            pltpu.VMEM((count, width), jnp.int32),
            pltpu.SemaphoreType.DMA((3, PARTS)),
        ]
        return pl.pallas_call(
            functools.partial(leaf_kernel, places),
            in_specs=[IN_VMEM if chunk else IN_ANY] * 3 + [IN_ANY] * (1 + len(fetches)),
            out_specs=[IN_VMEM] * (2 + len(fetches)),
            out_shape=[half(chunk)] * 2 + shapes,
            scratch_shapes=scratch + sems,
            cost_estimate=pl.CostEstimate(
                flops=4 * count * columns * degrees * width,
                bytes_accessed=2 * count * degrees * (columns + width),
                transcendentals=0,
            ),
            compiler_params=params,
            name="leaf",
        )(*inputs, after, *sources)

    def level(chunk, num, own, came, maps, after, fetches):
        count = sizes[chunk]
        sources, places, shapes, sems = fetched(fetches)
        return pl.pallas_call(
            functools.partial(level_kernel, firsts[chunk], num, places),
            in_specs=[IN_VMEM] * 3 + [IN_ANY] * (1 + len(fetches)),
            out_specs=[IN_VMEM] * (2 + len(fetches)),
            out_shape=[half(chunk)] * 2 + shapes,
            scratch_shapes=sems,
            cost_estimate=pl.CostEstimate(
                flops=2 * count * columns * width * width,
                bytes_accessed=2 * count * width * (width + 2 * columns),
                transcendentals=0,
            ),
            compiler_params=params,
            name="level",
        )(own, came, maps, after, *sources)

    def last(chunk, own, came, maps, lats, after):
        count = sizes[chunk]
        piece = jax.ShapeDtypeStruct((fields // peers, 2, count, rows), jnp.bfloat16)
        return pl.pallas_call(
            functools.partial(last_kernel, firsts[chunk], levels - 1),
            in_specs=[IN_VMEM] * 4 + [IN_ANY],
            out_specs=[IN_VMEM] * peers,
            out_shape=[piece] * peers,
            scratch_shapes=[pltpu.VMEM((count, columns, rows), jnp.bfloat16)],
            cost_estimate=pl.CostEstimate(
                flops=2 * count * columns * width * (width + rows),
                bytes_accessed=2 * count * width * (width + rows + 2 * columns),
                transcendentals=0,
            ),
            compiler_params=params,
            name="last",
        )(own, came, maps, lats, after)

    whole = [coef, leaf_map, skeleton]
    state, before, inputs = [], stay(skeleton), [stay(array) for array in whole]
    for chunk in chunks:
        if chunk + 1 < len(sizes):
            ahead = slice(firsts[chunk + 1], firsts[chunk + 1] + sizes[chunk + 1])
            fetches = [(array, ahead) for array in whole]
        else:
            fetches = [(level_maps, 0)]
        before, send, *inputs = leaf(chunk, inputs, before, fetches)
        state.append((before, exchange(send, "deg", 1)))
    maps = {0: inputs[0]}
    wanted = [(level_maps, num) for num in range(1, levels)] + [(lat_map, slice(0, slots))]
    for num in range(levels - 1):
        for chunk in chunks:
            fetches = [wanted[len(maps) - 1]] if len(maps) <= len(wanted) else []
            before, send, *more = level(chunk, num, *state[chunk], maps[num], before, fetches)
            maps.update({len(maps): array for array in more})
            state[chunk] = before, exchange(send, "deg", 2 << num)
    before = table = wave_table(wavemap, slots, sizes, NLON, before)
    blocks = []
    for chunk in chunks:
        pieces = last(chunk, *state[chunk], maps[levels - 1], maps[levels], before)
        before = pieces[0]
        blocks += [p if step == 0 else exchange(p, "wave", step) for step, p in enumerate(pieces)]
    return synthesis(blocks, table, NLON)


def solution(mesh):
    placed = (
        P("wave", None, None, "deg"),
        P("wave", "deg", None),
        P(None, "wave", "deg", None),
        P("wave", None, "deg"),
        P("wave", "deg"),
        P(),
    )
    return jax.shard_map(
        body, mesh=mesh, in_specs=placed, out_specs=P("wave", "deg", None), check_vma=False
    )
```

```python
import functools

import jax
import jax.numpy as jnp
from jax import lax
from jax.experimental import pallas as pl
from jax.experimental.pallas import tpu as pltpu
from jax.sharding import PartitionSpec as P

NLON = 8192
SHARES = (1, 1, 1, 1)
GROUPS = ((0, 1), (2, 3))
TURN = -1
BLOCK = 64
TABLE_STAGE = 2
TABLE_CHUNK = 2
LANES = 128
PARTS = 4
TILE = 512
ROWS = 256
SLOTS = 3
CHEAP = pl.CostEstimate(flops=0, bytes_accessed=0, transcendentals=0)
IN_ANY = pl.BlockSpec(memory_space=pl.ANY)
IN_VMEM = pl.BlockSpec(memory_space=pltpu.VMEM)


def stay(array):
    return pltpu.with_memory_space_constraint(array, pltpu.HBM)


def exchange(shard, axis, step):
    return lax.ppermute(shard, axis, [(i, i ^ step) for i in range(lax.axis_size(axis))])


def low_lanes(rows, width):
    return lax.broadcasted_iota(jnp.int32, (rows, width), 1) < width // 2


def split_halves(state):
    fields, width = state.shape[0] // 2, state.shape[1]
    real, imag = state[:fields], state[fields:]
    low = low_lanes(fields, width)
    first = jnp.where(low, real, pltpu.roll(imag, width // 2, 1))
    second = jnp.where(low, pltpu.roll(real, width // 2, 1), imag)
    return first.astype(jnp.bfloat16), second.astype(jnp.bfloat16)


def join_halves(first, second):
    fields, width = first.shape
    low = low_lanes(fields, width)
    first, second = first.astype(jnp.float32), second.astype(jnp.float32)
    real = jnp.where(low, first, pltpu.roll(second, width // 2, 1))
    imag = jnp.where(low, pltpu.roll(first, width // 2, 1), second)
    return jnp.concatenate([real, imag], 0).astype(jnp.bfloat16)


def dot(a, b):
    return jnp.dot(a, b, preferred_element_type=jnp.float32)


def upper_bit(level):
    return lax.axis_index("deg") >> level & 1


def put_halves(upper, state, own_ref, send_ref, g):
    first, second = split_halves(state)
    own_ref[g] = jnp.where(upper == 1, second, first)
    send_ref[g] = jnp.where(upper == 1, first, second)


def joined_state(upper, own_ref, came_ref, g):
    own, came = own_ref[g], came_ref[g]
    return join_halves(jnp.where(upper == 1, came, own), jnp.where(upper == 1, own, came))


def load_parts(source, target, sems):
    part = target.shape[0] // PARTS
    copies = []
    for n in range(PARTS):
        here = pl.ds(n * part, part)
        copies.append(pltpu.make_async_copy(source.at[here], target.at[here], sems.at[n]))
        copies[-1].start()
    return copies


def start_fetches(places, sources, targets, sems):
    copies = []
    for n, (place, source, target) in enumerate(zip(places, sources, targets)):
        copies.append(pltpu.make_async_copy(source.at[place], target, sems.at[n]))
        copies[-1].start()
    return copies


def leaf_kernel(places, *refs):
    fetches = len(places)
    coef, maps, skel, _, *sources = refs[: 4 + fetches]
    own_ref, send_ref, *targets = refs[4 + fetches : 6 + 2 * fetches]
    count, _, width = own_ref.shape
    degrees = maps.shape[1]
    scratch = refs[6 + 2 * fetches :]
    parts = []
    if len(scratch) > 3:
        coef_hbm, map_hbm, skel_hbm = coef, maps, skel
        coef, maps, skel, sems = scratch[:4]
        skel_copy = pltpu.make_async_copy(skel_hbm.at[pl.ds(0, count)], skel, sems.at[2, 0])
        skel_copy.start()
        parts = [load_parts(map_hbm, maps, sems.at[0]), load_parts(coef_hbm, coef, sems.at[1])]
    later = start_fetches(places, sources, targets, scratch[-1]) if fetches else []
    if parts:
        skel_copy.wait()
    rows = lax.broadcasted_iota(jnp.int32, (degrees, width), 0)
    for g in range(count):
        for copies in parts:
            if g % (count // PARTS) == 0:
                copies[g // (count // PARTS)].wait()
        picks = (rows == skel[g : g + 1, :]).astype(jnp.bfloat16)
        both = dot(coef[g], jnp.concatenate([maps[g], picks], 1))
        put_halves(upper_bit(0), both[:, :width] + both[:, width:], own_ref, send_ref, g)
    for copy in later:
        copy.wait()


def level_kernel(first, num, places, *refs):
    fetches = len(places)
    own_in, came_in, maps, _, *sources = refs[: 4 + fetches]
    own_ref, send_ref, *targets = refs[4 + fetches : 6 + 2 * fetches]
    later = start_fetches(places, sources, targets, refs[-1]) if fetches else []
    for g in range(own_in.shape[0]):
        joined = joined_state(upper_bit(num), own_in, came_in, g)
        put_halves(upper_bit(num + 1), dot(joined, maps[num, first + g]), own_ref, send_ref, g)
    for copy in later:
        copy.wait()


def last_kernel(first, num, offset, own_in, came_in, maps, lats, _, *refs):
    peers = lax.axis_size("wave")
    out_refs, block_ref = refs[-1 - peers : -1], refs[-1]
    count, fields = own_in.shape[:2]
    share = fields // peers
    for g in range(count):
        joined = joined_state(upper_bit(num), own_in, came_in, g)
        node = dot(joined, maps[num, first + g]).astype(jnp.bfloat16)
        block_ref[g] = dot(node, lats[first + g]).astype(jnp.bfloat16)
    tile = 16
    size = tile * tile
    out_at = lax.broadcasted_iota(jnp.int32, (size, size), 0)
    in_at = lax.broadcasted_iota(jnp.int32, (size, size), 1)
    swap = ((out_at // tile == in_at % tile) & (out_at % tile == in_at // tile)).astype(jnp.bfloat16)
    rows = block_ref.shape[2]
    me = lax.axis_index("wave")
    for g in range(0, count, tile):
        for c in range(0, 2 * fields, tile):
            moved = dot(swap, block_ref[g : g + tile, c : c + tile, :].reshape(size, rows)).astype(jnp.bfloat16)
            moved = moved.reshape(tile, tile, rows)
            part, field = c // fields, c % fields
            for at in range(0, tile, share):
                peer = (field + at) // share
                for step in range(peers):

                    @pl.when((me ^ peer) == step)
                    def _():
                        out_refs[step][:, part, offset + g : offset + g + tile, :] = moved[at : at + share]


def table_kernel(lon_count, slots, sizes, map_ref, after_ref, table_ref, q_ref):
    me = lax.axis_index("wave")
    row = 0
    for n, size in enumerate(sizes):
        for step in range(map_ref.shape[0] // slots):
            start = (me ^ step) * slots + sum(sizes[:n])

            def put(m, carry, row=row, start=start):
                q_ref[pl.ds(row + m, 1), :] = jnp.full((1, LANES), map_ref[start + m], jnp.int32)
                return carry

            lax.fori_loop(0, size, put, 0, unroll=8)
            row += size
    scale = 2.0 * jnp.pi / lon_count
    lane = lax.broadcasted_iota(jnp.int32, (BLOCK, LANES), 1)

    def rows(i, carry):
        here = pl.ds(pl.multiple_of(i * BLOCK, BLOCK), BLOCK)
        q = q_ref[here, :]
        low = (q * lane & lon_count - 1).astype(jnp.float32) * scale
        high = (q * (lane * LANES) & lon_count - 1).astype(jnp.float32) * scale
        weight = jnp.where(q == 0, 1.0, 2.0).astype(jnp.float32)
        cl, sl = jnp.cos(low) * weight, jnp.sin(low) * -weight
        ch, sh = jnp.cos(high), jnp.sin(high)
        for h in range(table_ref.shape[2] // LANES):
            c, s = ch[:, h : h + 1], sh[:, h : h + 1]
            table_ref[0, here, h * LANES : (h + 1) * LANES] = (c * cl + s * sl).astype(jnp.bfloat16)
            table_ref[1, here, h * LANES : (h + 1) * LANES] = (c * sl - s * cl).astype(jnp.bfloat16)
        return carry

    lax.fori_loop(0, q_ref.shape[0] // BLOCK, rows, 0)


def wave_table(wavemap, slots, sizes, lon_count, after):
    total = wavemap.shape[0]
    return pl.pallas_call(
        functools.partial(table_kernel, lon_count, slots, sizes),
        in_specs=[pl.BlockSpec(memory_space=pltpu.SMEM), IN_ANY],
        out_specs=IN_VMEM,
        out_shape=jax.ShapeDtypeStruct((2, total, lon_count // 2 + LANES), jnp.bfloat16),
        scratch_shapes=[pltpu.VMEM((total, LANES), jnp.int32)],
        cost_estimate=CHEAP,
        compiler_params=pltpu.CompilerParams(vmem_limit_bytes=16 * 2**20),
        name="table",
    )(wavemap, after)


def synthesis_kernel(*refs):
    block_refs = refs[:-6]
    table_ref, out_ref, left_ref, carry_ref, buffer_ref, sems = refs[-6:]
    fields, rows, lon_count = out_ref.shape
    slots, width = buffer_ref.shape[0], buffer_ref.shape[-1]
    for f in range(fields):
        for p in range(2):
            left_ref[p, f * rows : (f + 1) * rows, :] = jnp.concatenate([ref[f, p] for ref in block_refs], 0).T
    middle = pl.ds(lon_count // 2, LANES)
    carry_ref[...] = dot(left_ref[0], table_ref[0, :, middle]) - dot(left_ref[1], table_ref[1, :, middle])
    tiles = lon_count // width
    steps = tiles // 2
    size = ROWS
    lane = lax.broadcasted_iota(jnp.int32, (size, LANES), 1)
    mirror = (LANES - lane) % LANES

    def copies(i):
        slot, at = i % slots, steps - 1 - i
        straight = pl.ds(pl.multiple_of(at * width, width), width)
        turned = pl.ds(pl.multiple_of((tiles - 1 - at) * width, width), width)
        return (
            pltpu.make_async_copy(buffer_ref.at[slot, 0], out_ref.at[:, :, straight], sems.at[slot, 0]),
            pltpu.make_async_copy(buffer_ref.at[slot, 1], out_ref.at[:, :, turned], sems.at[slot, 1]),
        )

    def step(i, carry):
        slot, at = i % slots, steps - 1 - i
        straight = pl.ds(pl.multiple_of(at * width, width), width)

        @pl.when(i >= slots)
        def _():
            for copy in copies(i - slots):
                copy.wait()

        for r in range(0, fields * rows, size):
            f = r // rows
            n = size // rows
            cos_sum = dot(left_ref[0, r : r + size, :], table_ref[0, :, straight])
            sin_sum = dot(left_ref[1, r : r + size, :], table_ref[1, :, straight])
            buffer_ref[slot, 0, f : f + n] = (cos_sum + sin_sum).astype(jnp.bfloat16).reshape(n, rows, width)
            back = cos_sum - sin_sum
            following = carry_ref[r : r + size, :]
            for t in reversed(range(width // LANES)):
                piece = back[:, t * LANES : (t + 1) * LANES]
                turned = jnp.take_along_axis(piece, mirror, axis=1, mode="promise_in_bounds")
                turned = jnp.where(lane == 0, following, turned).astype(jnp.bfloat16)
                to = width - (t + 1) * LANES
                buffer_ref[slot, 1, f : f + n, :, to : to + LANES] = turned.reshape(n, rows, LANES)
                following = piece
            carry_ref[r : r + size, :] = following
        for copy in copies(i):
            copy.start()
        return carry

    lax.fori_loop(0, steps, step, 0)
    for i in range(max(0, steps - slots), steps):
        for copy in copies(i):
            copy.wait()


def synthesis(blocks, table, lon_count):
    fields, _, _, rows = blocks[0].shape
    depth = table.shape[1]
    return pl.pallas_call(
        synthesis_kernel,
        in_specs=[IN_VMEM] * (len(blocks) + 1),
        out_specs=pl.BlockSpec(memory_space=pl.ANY),
        out_shape=jax.ShapeDtypeStruct((fields, rows, lon_count), jnp.bfloat16),
        scratch_shapes=[
            pltpu.VMEM((2, fields * rows, depth), jnp.bfloat16),
            pltpu.VMEM((fields * rows, LANES), jnp.float32),
            pltpu.VMEM((SLOTS, 2, fields, rows, TILE), jnp.bfloat16),
            pltpu.SemaphoreType.DMA((SLOTS, 2)),
        ],
        cost_estimate=CHEAP,
        compiler_params=pltpu.CompilerParams(vmem_limit_bytes=32 * 2**20),
        name="synthesis",
    )(*blocks, table)


def body(spectrum, leaf_map, level_maps, lat_map, skeleton, wavemap):
    slots, _, fields, degrees = spectrum.shape
    columns = 2 * fields
    width = leaf_map.shape[2]
    levels = level_maps.shape[0]
    rows = lat_map.shape[2]
    coef = spectrum.reshape(slots, columns, degrees)
    peers = lax.axis_size("wave")
    sizes = [slots * share // sum(SHARES) for share in SHARES]
    firsts = [sum(sizes[:n]) for n in range(len(sizes))]
    chunks = range(len(sizes))
    params = pltpu.CompilerParams(vmem_limit_bytes=16 * 2**20)

    def half(chunk):
        return jax.ShapeDtypeStruct((sizes[chunk], fields, width), jnp.bfloat16)

    def fetched(fetches):
        shapes = []
        for array, place in fetches:
            view = jax.eval_shape(lambda a, place=place: a[place], array)
            shapes.append(jax.ShapeDtypeStruct(view.shape, view.dtype))
        sems = [pltpu.SemaphoreType.DMA((len(fetches),))] if fetches else []
        return [stay(array) for array, _ in fetches], [at(place) for _, place in fetches], shapes, sems

    def at(place):
        return pl.ds(place.start, place.stop - place.start) if isinstance(place, slice) else place

    def leaf(chunk, inputs, after, fetches):
        count = sizes[chunk]
        sources, places, shapes, sems = fetched(fetches)
        scratch = [] if chunk else [
            pltpu.VMEM((count, columns, degrees), jnp.bfloat16),
            pltpu.VMEM((count, degrees, width), jnp.bfloat16),
            pltpu.VMEM((count, width), jnp.int32),
            pltpu.SemaphoreType.DMA((3, PARTS)),
        ]
        return pl.pallas_call(
            functools.partial(leaf_kernel, places),
            in_specs=[IN_VMEM if chunk else IN_ANY] * 3 + [IN_ANY] * (1 + len(fetches)),
            out_specs=[IN_VMEM] * (2 + len(fetches)),
            out_shape=[half(chunk)] * 2 + shapes,
            scratch_shapes=scratch + sems,
            cost_estimate=CHEAP,
            compiler_params=params,
            name="leaf",
        )(*inputs, after, *sources)

    def level(chunk, num, own, came, maps, after, fetches):
        count = sizes[chunk]
        sources, places, shapes, sems = fetched(fetches)
        return pl.pallas_call(
            functools.partial(level_kernel, firsts[chunk], num, places),
            in_specs=[IN_VMEM] * 3 + [IN_ANY] * (1 + len(fetches)),
            out_specs=[IN_VMEM] * (2 + len(fetches)),
            out_shape=[half(chunk)] * 2 + shapes,
            scratch_shapes=sems,
            cost_estimate=CHEAP,
            compiler_params=params,
            name="level",
        )(own, came, maps, after, *sources)

    def last(chunk, own, came, maps, lats, after, group, begun):
        count = sizes[chunk]
        piece = jax.ShapeDtypeStruct((fields // peers, 2, sum(sizes[n] for n in group), rows), jnp.bfloat16)
        return pl.pallas_call(
            functools.partial(last_kernel, firsts[chunk], levels - 1, firsts[chunk] - firsts[group[0]]),
            in_specs=[IN_VMEM] * 4 + [IN_ANY] + [IN_VMEM] * len(begun),
            out_specs=[IN_VMEM] * peers,
            out_shape=[piece] * peers,
            input_output_aliases={5 + n: n for n in range(len(begun))},
            scratch_shapes=[pltpu.VMEM((count, columns, rows), jnp.bfloat16)],
            cost_estimate=CHEAP,
            compiler_params=params,
            name="last",
        )(own, came, maps, lats, after, *begun)

    whole = [coef, leaf_map, skeleton]
    order = [(chunk, stage) for chunk in chunks for stage in range(levels + 1)]
    order.sort(key=lambda turn: (sum(turn), TURN * turn[0]))
    wanted = []
    for chunk, stage in order:
        if stage == 0 and chunk:
            ahead = slice(firsts[chunk], firsts[chunk] + sizes[chunk])
            wanted.append((("leaf", chunk), [(array, ahead) for array in whole]))
    wanted.reverse()
    held = {("leaf", 0): [stay(array) for array in whole]}
    before, table = stay(skeleton), None
    state, begun, blocks = {}, [], []
    for chunk, stage in order:
        name, fetches = wanted.pop() if wanted else (None, [])
        if stage == TABLE_STAGE and chunk == TABLE_CHUNK:
            before = table = wave_table(wavemap, slots, [sum(sizes[n] for n in group) for group in GROUPS], NLON, before)
        if stage == levels:
            group = next(group for group in GROUPS if chunk in group)
            begun = last(chunk, *state[chunk], level_maps, lat_map, before, group, begun)
            before = begun[0]
            if chunk == group[-1]:
                blocks += [p if step == 0 else exchange(p, "wave", step) for step, p in enumerate(begun)]
                begun = []
            continue
        if stage == 0:
            before, send, *more = leaf(chunk, held["leaf", chunk], before, fetches)
        else:
            before, send, *more = level(chunk, stage - 1, *state[chunk], level_maps, before, fetches)
        held[name] = more
        state[chunk] = before, exchange(send, "deg", 1 << stage)
    return synthesis(blocks, table, NLON)


def solution(mesh):
    placed = (
        P("wave", None, None, "deg"),
        P("wave", "deg", None),
        P(None, "wave", "deg", None),
        P("wave", None, "deg"),
        P("wave", "deg"),
        P(),
    )
    return jax.shard_map(
        body, mesh=mesh, in_specs=placed, out_specs=P("wave", "deg", None), check_vma=False
    )
```

```python
import functools

import jax
import jax.numpy as jnp
from jax import lax
from jax.experimental import pallas as pl
from jax.experimental.pallas import tpu as pltpu
from jax.sharding import PartitionSpec as P

NLON = 8192
SHARES = (1, 1, 1, 1)
GROUPS = ((0, 1), (2, 3))
TURN = -1
BLOCK = 64
TABLE_AT = ()
LANES = 128
PARTS = 4
TILE = 512
ROWS = 256
SLOTS = 3
CHEAP = pl.CostEstimate(flops=0, bytes_accessed=0, transcendentals=0)
IN_ANY = pl.BlockSpec(memory_space=pl.ANY)
IN_VMEM = pl.BlockSpec(memory_space=pltpu.VMEM)


def stay(array):
    return pltpu.with_memory_space_constraint(array, pltpu.HBM)


def exchange(shard, axis, step):
    return lax.ppermute(shard, axis, [(i, i ^ step) for i in range(lax.axis_size(axis))])


def low_lanes(rows, width):
    return lax.broadcasted_iota(jnp.int32, (rows, width), 1) < width // 2


def split_halves(state):
    fields, width = state.shape[0] // 2, state.shape[1]
    real, imag = state[:fields], state[fields:]
    low = low_lanes(fields, width)
    first = jnp.where(low, real, pltpu.roll(imag, width // 2, 1))
    second = jnp.where(low, pltpu.roll(real, width // 2, 1), imag)
    return first.astype(jnp.bfloat16), second.astype(jnp.bfloat16)


def join_halves(first, second):
    fields, width = first.shape
    low = low_lanes(fields, width)
    first, second = first.astype(jnp.float32), second.astype(jnp.float32)
    real = jnp.where(low, first, pltpu.roll(second, width // 2, 1))
    imag = jnp.where(low, pltpu.roll(first, width // 2, 1), second)
    return jnp.concatenate([real, imag], 0).astype(jnp.bfloat16)


def dot(a, b):
    return jnp.dot(a, b, preferred_element_type=jnp.float32)


def upper_bit(level):
    return lax.axis_index("deg") >> level & 1


def put_halves(upper, state, own_ref, send_ref, g):
    first, second = split_halves(state)
    own_ref[g] = jnp.where(upper == 1, second, first)
    send_ref[g] = jnp.where(upper == 1, first, second)


def joined_state(upper, own_ref, came_ref, g):
    own, came = own_ref[g], came_ref[g]
    return join_halves(jnp.where(upper == 1, came, own), jnp.where(upper == 1, own, came))


def load_parts(source, target, sems):
    part = target.shape[0] // PARTS
    copies = []
    for n in range(PARTS):
        here = pl.ds(n * part, part)
        copies.append(pltpu.make_async_copy(source.at[here], target.at[here], sems.at[n]))
        copies[-1].start()
    return copies


def start_fetches(places, sources, targets, sems):
    copies = []
    for n, (place, source, target) in enumerate(zip(places, sources, targets)):
        copies.append(pltpu.make_async_copy(source.at[place], target, sems.at[n]))
        copies[-1].start()
    return copies


def leaf_kernel(places, *refs):
    fetches = len(places)
    coef, maps, skel, _, *sources = refs[: 4 + fetches]
    own_ref, send_ref, *targets = refs[4 + fetches : 6 + 2 * fetches]
    count, _, width = own_ref.shape
    degrees = maps.shape[1]
    scratch = refs[6 + 2 * fetches :]
    parts = []
    if len(scratch) > 3:
        coef_hbm, map_hbm, skel_hbm = coef, maps, skel
        coef, maps, skel, sems = scratch[:4]
        skel_copy = pltpu.make_async_copy(skel_hbm.at[pl.ds(0, count)], skel, sems.at[2, 0])
        skel_copy.start()
        parts = [load_parts(map_hbm, maps, sems.at[0]), load_parts(coef_hbm, coef, sems.at[1])]
    later = start_fetches(places, sources, targets, scratch[-1]) if fetches else []
    if parts:
        skel_copy.wait()
    rows = lax.broadcasted_iota(jnp.int32, (degrees, width), 0)
    for g in range(count):
        for copies in parts:
            if g % (count // PARTS) == 0:
                copies[g // (count // PARTS)].wait()
        picks = (rows == skel[g : g + 1, :]).astype(jnp.bfloat16)
        both = dot(coef[g], jnp.concatenate([maps[g], picks], 1))
        put_halves(upper_bit(0), both[:, :width] + both[:, width:], own_ref, send_ref, g)
    for copy in later:
        copy.wait()


def level_kernel(first, num, places, *refs):
    fetches = len(places)
    own_in, came_in, maps, _, *sources = refs[: 4 + fetches]
    own_ref, send_ref, *targets = refs[4 + fetches : 6 + 2 * fetches]
    later = start_fetches(places, sources, targets, refs[-1]) if fetches else []
    for g in range(own_in.shape[0]):
        joined = joined_state(upper_bit(num), own_in, came_in, g)
        put_halves(upper_bit(num + 1), dot(joined, maps[num, first + g]), own_ref, send_ref, g)
    for copy in later:
        copy.wait()


def last_kernel(first, num, offset, own_in, came_in, maps, lats, _, *refs):
    peers = lax.axis_size("wave")
    out_refs, block_ref = refs[-1 - peers : -1], refs[-1]
    count, fields = own_in.shape[:2]
    share = fields // peers
    for g in range(count):
        joined = joined_state(upper_bit(num), own_in, came_in, g)
        node = dot(joined, maps[num, first + g]).astype(jnp.bfloat16)
        block_ref[g] = dot(node, lats[first + g]).astype(jnp.bfloat16)
    tile = 16
    size = tile * tile
    out_at = lax.broadcasted_iota(jnp.int32, (size, size), 0)
    in_at = lax.broadcasted_iota(jnp.int32, (size, size), 1)
    shift = tile.bit_length() - 1
    swap = (out_at >> shift) + ((out_at & tile - 1) << shift) == in_at
    swap = swap.astype(jnp.bfloat16)
    rows = block_ref.shape[2]
    me = lax.axis_index("wave")
    for g in range(0, count, tile):
        for c in range(0, 2 * fields, tile):
            moved = dot(swap, block_ref[g : g + tile, c : c + tile, :].reshape(size, rows)).astype(jnp.bfloat16)
            moved = moved.reshape(tile, tile, rows)
            part, field = c // fields, c % fields
            for at in range(0, tile, share):
                peer = (field + at) // share
                for step in range(peers):

                    @pl.when((me ^ peer) == step)
                    def _():
                        out_refs[step][:, part, offset + g : offset + g + tile, :] = moved[at : at + share]


def table_kernel(lon_count, slots, sizes, first, count, map_ref, *refs):
    table_ref, q_ref = refs[-2:]
    me = lax.axis_index("wave")
    row = 0
    for n, size in enumerate(sizes):
        for step in range(map_ref.shape[0] // slots):
            start = (me ^ step) * slots + sum(sizes[:n])

            def put(m, carry, row=row, start=start):
                q_ref[pl.ds(row + m, 1), :] = jnp.full((1, LANES), map_ref[start + m], jnp.int32)
                return carry

            if first <= row < first + count:
                lax.fori_loop(0, size, put, 0, unroll=8)
            row += size
    scale = 2.0 * jnp.pi / lon_count
    lane = lax.broadcasted_iota(jnp.int32, (BLOCK, LANES), 1)

    def rows(i, carry):
        here = pl.ds(pl.multiple_of(i * BLOCK, BLOCK), BLOCK)
        q = q_ref[here, :]
        low = (q * lane & lon_count - 1).astype(jnp.float32) * scale
        high = (q * (lane * LANES) & lon_count - 1).astype(jnp.float32) * scale
        weight = jnp.where(q == 0, 1.0, 2.0).astype(jnp.float32)
        cl, sl = jnp.cos(low) * weight, jnp.sin(low) * -weight
        ch, sh = jnp.cos(high), jnp.sin(high)
        for h in range(table_ref.shape[2] // LANES):
            c, s = ch[:, h : h + 1], sh[:, h : h + 1]
            table_ref[0, here, h * LANES : (h + 1) * LANES] = (c * cl + s * sl).astype(jnp.bfloat16)
            table_ref[1, here, h * LANES : (h + 1) * LANES] = (c * sl - s * cl).astype(jnp.bfloat16)
        return carry

    lax.fori_loop(first // BLOCK, (first + count) // BLOCK, rows, 0)


def wave_table(wavemap, slots, sizes, lon_count, after, begun, first, count):
    total = wavemap.shape[0]
    return pl.pallas_call(
        functools.partial(table_kernel, lon_count, slots, sizes, first, count),
        in_specs=[pl.BlockSpec(memory_space=pltpu.SMEM), IN_ANY] + [IN_VMEM] * len(begun),
        input_output_aliases={2: 0} if begun else {},
        out_specs=IN_VMEM,
        out_shape=jax.ShapeDtypeStruct((2, total, lon_count // 2 + LANES), jnp.bfloat16),
        scratch_shapes=[pltpu.VMEM((total, LANES), jnp.int32)],
        cost_estimate=CHEAP,
        compiler_params=pltpu.CompilerParams(vmem_limit_bytes=16 * 2**20),
        name="table",
    )(wavemap, after, *begun)


def synthesis_kernel(*refs):
    block_refs = refs[:-6]
    table_ref, out_ref, left_ref, carry_ref, buffer_ref, sems = refs[-6:]
    fields, rows, lon_count = out_ref.shape
    slots, width = buffer_ref.shape[0], buffer_ref.shape[-1]
    for f in range(fields):
        for p in range(2):
            left_ref[p, f * rows : (f + 1) * rows, :] = jnp.concatenate([ref[f, p] for ref in block_refs], 0).T
    middle = pl.ds(lon_count // 2, LANES)
    carry_ref[...] = dot(left_ref[0], table_ref[0, :, middle]) - dot(left_ref[1], table_ref[1, :, middle])
    tiles = lon_count // width
    steps = tiles // 2
    size = ROWS
    lane = lax.broadcasted_iota(jnp.int32, (size, LANES), 1)
    mirror = (LANES - lane) % LANES

    def copies(i):
        slot, at = i % slots, steps - 1 - i
        straight = pl.ds(pl.multiple_of(at * width, width), width)
        turned = pl.ds(pl.multiple_of((tiles - 1 - at) * width, width), width)
        return (
            pltpu.make_async_copy(buffer_ref.at[slot, 0], out_ref.at[:, :, straight], sems.at[slot, 0]),
            pltpu.make_async_copy(buffer_ref.at[slot, 1], out_ref.at[:, :, turned], sems.at[slot, 1]),
        )

    def step(i, carry):
        slot, at = i % slots, steps - 1 - i
        straight = pl.ds(pl.multiple_of(at * width, width), width)

        @pl.when(i >= slots)
        def _():
            for copy in copies(i - slots):
                copy.wait()

        for r in range(0, fields * rows, size):
            f = r // rows
            n = size // rows
            cos_sum = dot(left_ref[0, r : r + size, :], table_ref[0, :, straight])
            sin_sum = dot(left_ref[1, r : r + size, :], table_ref[1, :, straight])
            buffer_ref[slot, 0, f : f + n] = (cos_sum + sin_sum).astype(jnp.bfloat16).reshape(n, rows, width)
            back = cos_sum - sin_sum
            following = carry_ref[r : r + size, :]
            for t in reversed(range(width // LANES)):
                piece = back[:, t * LANES : (t + 1) * LANES]
                turned = jnp.take_along_axis(piece, mirror, axis=1, mode="promise_in_bounds")
                turned = jnp.where(lane == 0, following, turned).astype(jnp.bfloat16)
                to = width - (t + 1) * LANES
                buffer_ref[slot, 1, f : f + n, :, to : to + LANES] = turned.reshape(n, rows, LANES)
                following = piece
            carry_ref[r : r + size, :] = following
        for copy in copies(i):
            copy.start()
        return carry

    lax.fori_loop(0, steps, step, 0)
    for i in range(max(0, steps - slots), steps):
        for copy in copies(i):
            copy.wait()


def synthesis(blocks, table, lon_count):
    fields, _, _, rows = blocks[0].shape
    depth = table.shape[1]
    return pl.pallas_call(
        synthesis_kernel,
        in_specs=[IN_VMEM] * (len(blocks) + 1),
        out_specs=pl.BlockSpec(memory_space=pl.ANY),
        out_shape=jax.ShapeDtypeStruct((fields, rows, lon_count), jnp.bfloat16),
        scratch_shapes=[
            pltpu.VMEM((2, fields * rows, depth), jnp.bfloat16),
            pltpu.VMEM((fields * rows, LANES), jnp.float32),
            pltpu.VMEM((SLOTS, 2, fields, rows, TILE), jnp.bfloat16),
            pltpu.SemaphoreType.DMA((SLOTS, 2)),
        ],
        cost_estimate=CHEAP,
        compiler_params=pltpu.CompilerParams(vmem_limit_bytes=32 * 2**20),
        name="synthesis",
    )(*blocks, table)


def body(spectrum, leaf_map, level_maps, lat_map, skeleton, wavemap):
    slots, _, fields, degrees = spectrum.shape
    columns = 2 * fields
    width = leaf_map.shape[2]
    levels = level_maps.shape[0]
    rows = lat_map.shape[2]
    coef = spectrum.reshape(slots, columns, degrees)
    peers = lax.axis_size("wave")
    sizes = [slots * share // sum(SHARES) for share in SHARES]
    firsts = [sum(sizes[:n]) for n in range(len(sizes))]
    chunks = range(len(sizes))
    params = pltpu.CompilerParams(vmem_limit_bytes=16 * 2**20)

    def half(chunk):
        return jax.ShapeDtypeStruct((sizes[chunk], fields, width), jnp.bfloat16)

    def fetched(fetches):
        shapes = []
        for array, place in fetches:
            view = jax.eval_shape(lambda a, place=place: a[place], array)
            shapes.append(jax.ShapeDtypeStruct(view.shape, view.dtype))
        sems = [pltpu.SemaphoreType.DMA((len(fetches),))] if fetches else []
        return [stay(array) for array, _ in fetches], [at(place) for _, place in fetches], shapes, sems

    def at(place):
        return pl.ds(place.start, place.stop - place.start) if isinstance(place, slice) else place

    def leaf(chunk, inputs, after, fetches):
        count = sizes[chunk]
        sources, places, shapes, sems = fetched(fetches)
        scratch = [] if chunk else [
            pltpu.VMEM((count, columns, degrees), jnp.bfloat16),
            pltpu.VMEM((count, degrees, width), jnp.bfloat16),
            pltpu.VMEM((count, width), jnp.int32),
            pltpu.SemaphoreType.DMA((3, PARTS)),
        ]
        return pl.pallas_call(
            functools.partial(leaf_kernel, places),
            in_specs=[IN_VMEM if chunk else IN_ANY] * 3 + [IN_ANY] * (1 + len(fetches)),
            out_specs=[IN_VMEM] * (2 + len(fetches)),
            out_shape=[half(chunk)] * 2 + shapes,
            scratch_shapes=scratch + sems,
            cost_estimate=CHEAP,
            compiler_params=params,
            name="leaf",
        )(*inputs, after, *sources)

    def level(chunk, num, own, came, maps, after, fetches):
        count = sizes[chunk]
        sources, places, shapes, sems = fetched(fetches)
        return pl.pallas_call(
            functools.partial(level_kernel, firsts[chunk], num, places),
            in_specs=[IN_VMEM] * 3 + [IN_ANY] * (1 + len(fetches)),
            out_specs=[IN_VMEM] * (2 + len(fetches)),
            out_shape=[half(chunk)] * 2 + shapes,
            scratch_shapes=sems,
            cost_estimate=CHEAP,
            compiler_params=params,
            name="level",
        )(own, came, maps, after, *sources)

    def last(chunk, own, came, maps, lats, after, group, begun):
        count = sizes[chunk]
        piece = jax.ShapeDtypeStruct((fields // peers, 2, sum(sizes[n] for n in group), rows), jnp.bfloat16)
        return pl.pallas_call(
            functools.partial(last_kernel, firsts[chunk], levels - 1, firsts[chunk] - firsts[group[0]]),
            in_specs=[IN_VMEM] * 4 + [IN_ANY] + [IN_VMEM] * len(begun),
            out_specs=[IN_VMEM] * peers,
            out_shape=[piece] * peers,
            input_output_aliases={5 + n: n for n in range(len(begun))},
            scratch_shapes=[pltpu.VMEM((count, columns, rows), jnp.bfloat16)],
            cost_estimate=CHEAP,
            compiler_params=params,
            name="last",
        )(own, came, maps, lats, after, *begun)

    whole = [coef, leaf_map, skeleton]
    order = [(chunk, stage) for chunk in chunks for stage in range(levels + 1)]
    order.sort(key=lambda turn: (sum(turn), TURN * turn[0]))
    wanted = []
    for chunk, stage in order:
        if stage == 0 and chunk:
            ahead = slice(firsts[chunk], firsts[chunk] + sizes[chunk])
            wanted.append((("leaf", chunk), [(array, ahead) for array in whole]))
    wanted.reverse()
    held = {("leaf", 0): [stay(array) for array in whole]}
    before, table, filled = stay(skeleton), None, 0
    group_sizes = [sum(sizes[n] for n in group) for group in GROUPS]
    share_rows = slots * peers // (1 + len(TABLE_AT))

    def make_table(after, table):
        nonlocal filled
        begun = [] if table is None else [table]
        filled += share_rows
        return wave_table(wavemap, slots, group_sizes, NLON, after, begun, filled - share_rows, share_rows)

    state, begun, blocks = {}, [], []
    for chunk, stage in order:
        name, fetches = wanted.pop() if wanted else (None, [])
        if (chunk, stage) in TABLE_AT:
            before = table = make_table(before, table)
        if stage == levels:
            group = next(group for group in GROUPS if chunk in group)
            begun = last(chunk, *state[chunk], level_maps, lat_map, before, group, begun)
            before = begun[0]
            if chunk == group[-1]:
                blocks += [p if step == 0 else exchange(p, "wave", step) for step, p in enumerate(begun)]
                begun = []
            continue
        if stage == 0:
            before, send, *more = leaf(chunk, held["leaf", chunk], before, fetches)
        else:
            before, send, *more = level(chunk, stage - 1, *state[chunk], level_maps, before, fetches)
        held[name] = more
        state[chunk] = before, exchange(send, "deg", 1 << stage)
    while filled < slots * peers:
        before = table = make_table(before, table)
    return synthesis(blocks, table, NLON)


def solution(mesh):
    placed = (
        P("wave", None, None, "deg"),
        P("wave", "deg", None),
        P(None, "wave", "deg", None),
        P("wave", None, "deg"),
        P("wave", "deg"),
        P(),
    )
    return jax.shard_map(
        body, mesh=mesh, in_specs=placed, out_specs=P("wave", "deg", None), check_vma=False
    )
```

```python
import functools

import jax
import jax.numpy as jnp
from jax import lax
from jax.experimental import pallas as pl
from jax.experimental.pallas import tpu as pltpu
from jax.sharding import PartitionSpec as P

NLON = 8192
SHARES = (1, 1, 1, 1)
GROUPS = ((0, 1), (2,), (3,))
TURN = -1
BLOCK = 64
TABLE_AT = ((3, 3),)
LANES = 128
PARTS = 2
TILE = 512
ROWS = 256
SLOTS = 3
UNROLL = 4
CHEAP = pl.CostEstimate(flops=0, bytes_accessed=0, transcendentals=0)
IN_ANY = pl.BlockSpec(memory_space=pl.ANY)
IN_VMEM = pl.BlockSpec(memory_space=pltpu.VMEM)


def stay(array):
    return pltpu.with_memory_space_constraint(array, pltpu.HBM)


def exchange(shard, axis, step):
    return lax.ppermute(shard, axis, [(i, i ^ step) for i in range(lax.axis_size(axis))])


def low_lanes(rows, width):
    return lax.broadcasted_iota(jnp.int32, (rows, width), 1) < width // 2


def split_halves(state):
    fields, width = state.shape[0] // 2, state.shape[1]
    real, imag = state[:fields], state[fields:]
    low = low_lanes(fields, width)
    first = jnp.where(low, real, pltpu.roll(imag, width // 2, 1))
    second = jnp.where(low, pltpu.roll(real, width // 2, 1), imag)
    return first.astype(jnp.bfloat16), second.astype(jnp.bfloat16)


def join_halves(first, second):
    fields, width = first.shape
    low = low_lanes(fields, width)
    first, second = first.astype(jnp.float32), second.astype(jnp.float32)
    real = jnp.where(low, first, pltpu.roll(second, width // 2, 1))
    imag = jnp.where(low, pltpu.roll(first, width // 2, 1), second)
    return jnp.concatenate([real, imag], 0).astype(jnp.bfloat16)


def dot(a, b):
    return jnp.dot(a, b, preferred_element_type=jnp.float32)


def upper_bit(level):
    return lax.axis_index("deg") >> level & 1


def put_halves(upper, state, own_ref, send_ref, g):
    first, second = split_halves(state)
    own_ref[g] = jnp.where(upper == 1, second, first)
    send_ref[g] = jnp.where(upper == 1, first, second)


def joined_state(upper, own_ref, came_ref, g):
    own, came = own_ref[g], came_ref[g]
    return join_halves(jnp.where(upper == 1, came, own), jnp.where(upper == 1, own, came))


def load_parts(source, target, sems):
    part = target.shape[0] // PARTS
    copies = []
    for n in range(PARTS):
        here = pl.ds(n * part, part)
        copies.append(pltpu.make_async_copy(source.at[here], target.at[here], sems.at[n]))
        copies[-1].start()
    return copies


def start_fetches(places, sources, targets, sems):
    copies = []
    for n, (place, source, target) in enumerate(zip(places, sources, targets)):
        copies.append(pltpu.make_async_copy(source.at[place], target, sems.at[n]))
        copies[-1].start()
    return copies


def leaf_kernel(places, *refs):
    fetches = len(places)
    coef, maps, skel, _, *sources = refs[: 4 + fetches]
    own_ref, send_ref, *targets = refs[4 + fetches : 6 + 2 * fetches]
    count, _, width = own_ref.shape
    degrees = maps.shape[1]
    scratch = refs[6 + 2 * fetches :]
    parts = []
    if len(scratch) > 3:
        coef_hbm, map_hbm, skel_hbm = coef, maps, skel
        coef, maps, skel, sems = scratch[:4]
        skel_copy = pltpu.make_async_copy(skel_hbm.at[pl.ds(0, count)], skel, sems.at[2, 0])
        skel_copy.start()
        parts = [load_parts(map_hbm, maps, sems.at[0]), load_parts(coef_hbm, coef, sems.at[1])]
    later = start_fetches(places, sources, targets, scratch[-1]) if fetches else []
    if parts:
        skel_copy.wait()
    rows = lax.broadcasted_iota(jnp.int32, (degrees, width), 0)
    for g in range(count):
        for copies in parts:
            if g % (count // PARTS) == 0:
                copies[g // (count // PARTS)].wait()
        picks = (rows == skel[g : g + 1, :]).astype(jnp.bfloat16)
        both = dot(coef[g], jnp.concatenate([maps[g], picks], 1))
        put_halves(upper_bit(0), both[:, :width] + both[:, width:], own_ref, send_ref, g)
    for copy in later:
        copy.wait()


def level_kernel(first, num, places, *refs):
    fetches = len(places)
    own_in, came_in, maps, _, *sources = refs[: 4 + fetches]
    own_ref, send_ref, *targets = refs[4 + fetches : 6 + 2 * fetches]
    later = start_fetches(places, sources, targets, refs[-1]) if fetches else []
    for g in range(own_in.shape[0]):
        joined = joined_state(upper_bit(num), own_in, came_in, g)
        put_halves(upper_bit(num + 1), dot(joined, maps[num, first + g]), own_ref, send_ref, g)
    for copy in later:
        copy.wait()


def last_kernel(first, num, offset, own_in, came_in, maps, lats, _, *refs):
    peers = lax.axis_size("wave")
    out_refs, (block_ref, moved_ref) = refs[-2 - peers : -2], refs[-2:]
    count, fields = own_in.shape[:2]
    share = fields // peers
    for g in range(count):
        joined = joined_state(upper_bit(num), own_in, came_in, g)
        node = dot(joined, maps[num, first + g]).astype(jnp.bfloat16)
        block_ref[g] = dot(node, lats[first + g]).astype(jnp.bfloat16)
    tile = 16
    size = tile * tile
    out_at = lax.broadcasted_iota(jnp.int32, (size, size), 0)
    in_at = lax.broadcasted_iota(jnp.int32, (size, size), 1)
    shift = tile.bit_length() - 1
    swap = (out_at >> shift) + ((out_at & tile - 1) << shift) == in_at
    swap = swap.astype(jnp.bfloat16)
    rows = block_ref.shape[2]
    me = lax.axis_index("wave")
    for g in range(0, count, tile):
        for c in range(0, 2 * fields, tile):
            moved = dot(swap, block_ref[g : g + tile, c : c + tile, :].reshape(size, rows)).astype(jnp.bfloat16)
            moved = moved.reshape(tile, tile, rows)
            part, field = c // fields, c % fields
            for at in range(0, tile, share):
                moved_ref[(field + at) // share, :, part, g : g + tile, :] = moved[at : at + share]
    for step, out_ref in enumerate(out_refs):
        out_ref[:, :, offset : offset + count, :] = moved_ref[me ^ step]


def table_kernel(lon_count, slots, sizes, first, count, map_ref, *refs):
    table_ref, q_ref = refs[-2:]
    me = lax.axis_index("wave")
    row = 0
    for n, size in enumerate(sizes):
        for step in range(map_ref.shape[0] // slots):
            start = (me ^ step) * slots + sum(sizes[:n])

            def put(m, carry, row=row, start=start):
                q_ref[pl.ds(row + m, 1), :] = jnp.full((1, LANES), map_ref[start + m], jnp.int32)
                return carry

            if first <= row < first + count:
                lax.fori_loop(0, size, put, 0, unroll=8)
            row += size
    scale = 2.0 * jnp.pi / lon_count
    lane = lax.broadcasted_iota(jnp.int32, (BLOCK, LANES), 1)

    def rows(i, carry):
        here = pl.ds(pl.multiple_of(i * BLOCK, BLOCK), BLOCK)
        q = q_ref[here, :]
        low = (q * lane & lon_count - 1).astype(jnp.float32) * scale
        high = (q * (lane * LANES) & lon_count - 1).astype(jnp.float32) * scale
        weight = jnp.where(q == 0, 1.0, 2.0).astype(jnp.float32)
        cl, sl = jnp.cos(low) * weight, jnp.sin(low) * -weight
        ch, sh = jnp.cos(high), jnp.sin(high)
        for h in range(table_ref.shape[2] // LANES):
            c, s = ch[:, h : h + 1], sh[:, h : h + 1]
            table_ref[0, here, h * LANES : (h + 1) * LANES] = (c * cl + s * sl).astype(jnp.bfloat16)
            table_ref[1, here, h * LANES : (h + 1) * LANES] = (c * sl - s * cl).astype(jnp.bfloat16)
        return carry

    lax.fori_loop(first // BLOCK, (first + count) // BLOCK, rows, 0)


def wave_table(wavemap, slots, sizes, lon_count, after, begun, first, count):
    total = wavemap.shape[0]
    return pl.pallas_call(
        functools.partial(table_kernel, lon_count, slots, sizes, first, count),
        in_specs=[pl.BlockSpec(memory_space=pltpu.SMEM), IN_ANY] + [IN_VMEM] * len(begun),
        input_output_aliases={2: 0} if begun else {},
        out_specs=IN_VMEM,
        out_shape=jax.ShapeDtypeStruct((2, total, lon_count // 2 + LANES), jnp.bfloat16),
        scratch_shapes=[pltpu.VMEM((total, LANES), jnp.int32)],
        cost_estimate=CHEAP,
        compiler_params=pltpu.CompilerParams(vmem_limit_bytes=16 * 2**20),
        name="table",
    )(wavemap, after, *begun)


def synthesis_kernel(*refs):
    block_refs = refs[:-6]
    table_ref, out_ref, left_ref, carry_ref, buffer_ref, sems = refs[-6:]
    fields, rows, lon_count = out_ref.shape
    slots, width = buffer_ref.shape[0], buffer_ref.shape[-1]
    for f in range(fields):
        for p in range(2):
            left_ref[p, f * rows : (f + 1) * rows, :] = jnp.concatenate([ref[f, p] for ref in block_refs], 0).T
    middle = pl.ds(lon_count // 2, LANES)
    carry_ref[...] = dot(left_ref[0], table_ref[0, :, middle]) - dot(left_ref[1], table_ref[1, :, middle])
    tiles = lon_count // width
    steps = tiles // 2
    size = ROWS
    lane = lax.broadcasted_iota(jnp.int32, (size, LANES), 1)
    mirror = (LANES - lane) % LANES

    def copies(i):
        slot, at = i % slots, steps - 1 - i
        straight = pl.ds(pl.multiple_of(at * width, width), width)
        turned = pl.ds(pl.multiple_of((tiles - 1 - at) * width, width), width)
        return (
            pltpu.make_async_copy(buffer_ref.at[slot, 0], out_ref.at[:, :, straight], sems.at[slot, 0]),
            pltpu.make_async_copy(buffer_ref.at[slot, 1], out_ref.at[:, :, turned], sems.at[slot, 1]),
        )

    def step(i, carry):
        slot, at = i % slots, steps - 1 - i
        straight = pl.ds(pl.multiple_of(at * width, width), width)

        @pl.when(i >= slots)
        def _():
            for copy in copies(i - slots):
                copy.wait()

        for r in range(0, fields * rows, size):
            f = r // rows
            n = size // rows
            cos_sum = dot(left_ref[0, r : r + size, :], table_ref[0, :, straight])
            sin_sum = dot(left_ref[1, r : r + size, :], table_ref[1, :, straight])
            buffer_ref[slot, 0, f : f + n] = (cos_sum + sin_sum).astype(jnp.bfloat16).reshape(n, rows, width)
            back = cos_sum - sin_sum
            following = carry_ref[r : r + size, :]
            for t in reversed(range(width // LANES)):
                piece = back[:, t * LANES : (t + 1) * LANES]
                turned = jnp.take_along_axis(piece, mirror, axis=1, mode="promise_in_bounds")
                turned = jnp.where(lane == 0, following, turned).astype(jnp.bfloat16)
                to = width - (t + 1) * LANES
                buffer_ref[slot, 1, f : f + n, :, to : to + LANES] = turned.reshape(n, rows, LANES)
                following = piece
            carry_ref[r : r + size, :] = following
        for copy in copies(i):
            copy.start()
        return carry

    lax.fori_loop(0, steps, step, 0, unroll=UNROLL)
    for i in range(max(0, steps - slots), steps):
        for copy in copies(i):
            copy.wait()


def synthesis(blocks, table, lon_count):
    fields, _, _, rows = blocks[0].shape
    depth = table.shape[1]
    return pl.pallas_call(
        synthesis_kernel,
        in_specs=[IN_VMEM] * (len(blocks) + 1),
        out_specs=pl.BlockSpec(memory_space=pl.ANY),
        out_shape=jax.ShapeDtypeStruct((fields, rows, lon_count), jnp.bfloat16),
        scratch_shapes=[
            pltpu.VMEM((2, fields * rows, depth), jnp.bfloat16),
            pltpu.VMEM((fields * rows, LANES), jnp.float32),
            pltpu.VMEM((SLOTS, 2, fields, rows, TILE), jnp.bfloat16),
            pltpu.SemaphoreType.DMA((SLOTS, 2)),
        ],
        cost_estimate=CHEAP,
        compiler_params=pltpu.CompilerParams(vmem_limit_bytes=32 * 2**20),
        name="synthesis",
    )(*blocks, table)


def body(spectrum, leaf_map, level_maps, lat_map, skeleton, wavemap):
    slots, _, fields, degrees = spectrum.shape
    columns = 2 * fields
    width = leaf_map.shape[2]
    levels = level_maps.shape[0]
    rows = lat_map.shape[2]
    coef = spectrum.reshape(slots, columns, degrees)
    peers = lax.axis_size("wave")
    sizes = [slots * share // sum(SHARES) for share in SHARES]
    firsts = [sum(sizes[:n]) for n in range(len(sizes))]
    chunks = range(len(sizes))
    params = pltpu.CompilerParams(vmem_limit_bytes=16 * 2**20)

    def half(chunk):
        return jax.ShapeDtypeStruct((sizes[chunk], fields, width), jnp.bfloat16)

    def fetched(fetches):
        shapes = []
        for array, place in fetches:
            view = jax.eval_shape(lambda a, place=place: a[place], array)
            shapes.append(jax.ShapeDtypeStruct(view.shape, view.dtype))
        sems = [pltpu.SemaphoreType.DMA((len(fetches),))] if fetches else []
        return [stay(array) for array, _ in fetches], [at(place) for _, place in fetches], shapes, sems

    def at(place):
        return pl.ds(place.start, place.stop - place.start) if isinstance(place, slice) else place

    def leaf(chunk, inputs, after, fetches):
        count = sizes[chunk]
        sources, places, shapes, sems = fetched(fetches)
        scratch = [] if chunk else [
            pltpu.VMEM((count, columns, degrees), jnp.bfloat16),
            pltpu.VMEM((count, degrees, width), jnp.bfloat16),
            pltpu.VMEM((count, width), jnp.int32),
            pltpu.SemaphoreType.DMA((3, PARTS)),
        ]
        return pl.pallas_call(
            functools.partial(leaf_kernel, places),
            in_specs=[IN_VMEM if chunk else IN_ANY] * 3 + [IN_ANY] * (1 + len(fetches)),
            out_specs=[IN_VMEM] * (2 + len(fetches)),
            out_shape=[half(chunk)] * 2 + shapes,
            scratch_shapes=scratch + sems,
            cost_estimate=CHEAP,
            compiler_params=params,
            name="leaf",
        )(*inputs, after, *sources)

    def level(chunk, num, own, came, maps, after, fetches):
        count = sizes[chunk]
        sources, places, shapes, sems = fetched(fetches)
        return pl.pallas_call(
            functools.partial(level_kernel, firsts[chunk], num, places),
            in_specs=[IN_VMEM] * 3 + [IN_ANY] * (1 + len(fetches)),
            out_specs=[IN_VMEM] * (2 + len(fetches)),
            out_shape=[half(chunk)] * 2 + shapes,
            scratch_shapes=sems,
            cost_estimate=CHEAP,
            compiler_params=params,
            name="level",
        )(own, came, maps, after, *sources)

    def last(chunk, own, came, maps, lats, after, group, begun):
        count = sizes[chunk]
        piece = jax.ShapeDtypeStruct((fields // peers, 2, sum(sizes[n] for n in group), rows), jnp.bfloat16)
        return pl.pallas_call(
            functools.partial(last_kernel, firsts[chunk], levels - 1, firsts[chunk] - firsts[group[0]]),
            in_specs=[IN_VMEM] * 4 + [IN_ANY] + [IN_VMEM] * len(begun),
            out_specs=[IN_VMEM] * peers,
            out_shape=[piece] * peers,
            input_output_aliases={5 + n: n for n in range(len(begun))},
            scratch_shapes=[
                pltpu.VMEM((count, columns, rows), jnp.bfloat16),
                pltpu.VMEM((peers, fields // peers, 2, count, rows), jnp.bfloat16),
            ],
            cost_estimate=CHEAP,
            compiler_params=params,
            name="last",
        )(own, came, maps, lats, after, *begun)

    whole = [coef, leaf_map, skeleton]
    order = [(chunk, stage) for chunk in chunks for stage in range(levels + 1)]
    order.sort(key=lambda turn: (sum(turn), TURN * turn[0]))
    wanted = []
    for chunk, stage in order:
        if stage == 0 and chunk:
            ahead = slice(firsts[chunk], firsts[chunk] + sizes[chunk])
            wanted.append((("leaf", chunk), [(array, ahead) for array in whole]))
    wanted.reverse()
    held = {("leaf", 0): [stay(array) for array in whole]}
    before, table, filled = stay(skeleton), None, 0
    group_sizes = [sum(sizes[n] for n in group) for group in GROUPS]
    share_rows = slots * peers // (1 + len(TABLE_AT))

    def make_table(after, table):
        nonlocal filled
        begun = [] if table is None else [table]
        filled += share_rows
        return wave_table(wavemap, slots, group_sizes, NLON, after, begun, filled - share_rows, share_rows)

    state, begun, blocks = {}, [], []
    for chunk, stage in order:
        name, fetches = wanted.pop() if wanted else (None, [])
        if (chunk, stage) in TABLE_AT:
            before = table = make_table(before, table)
        if stage == levels:
            group = next(group for group in GROUPS if chunk in group)
            begun = last(chunk, *state[chunk], level_maps, lat_map, before, group, begun)
            before = begun[0]
            if chunk == group[-1]:
                blocks += [p if step == 0 else exchange(p, "wave", step) for step, p in enumerate(begun)]
                begun = []
            continue
        if stage == 0:
            before, send, *more = leaf(chunk, held["leaf", chunk], before, fetches)
        else:
            before, send, *more = level(chunk, stage - 1, *state[chunk], level_maps, before, fetches)
        held[name] = more
        state[chunk] = before, exchange(send, "deg", 1 << stage)
    while filled < slots * peers:
        before = table = make_table(before, table)
    return synthesis(blocks, table, NLON)


def solution(mesh):
    placed = (
        P("wave", None, None, "deg"),
        P("wave", "deg", None),
        P(None, "wave", "deg", None),
        P("wave", None, "deg"),
        P("wave", "deg"),
        P(),
    )
    return jax.shard_map(
        body, mesh=mesh, in_specs=placed, out_specs=P("wave", "deg", None), check_vma=False
    )
```

```python
import functools

import jax
import jax.numpy as jnp
from jax import lax
from jax.experimental import pallas as pl
from jax.experimental.pallas import tpu as pltpu
from jax.sharding import PartitionSpec as P

NLON = 8192
SHARES = (1, 1, 1, 1)
GROUPS = ((0, 1), (2,), (3,))
TURN = -1
BLOCK = 64
TABLE_AT = ((3, 3),)
LANES = 128
PARTS = 2
TILE = 512
ROWS = 256
SLOTS = 3
UNROLL = 4
CHEAP = pl.CostEstimate(flops=0, bytes_accessed=0, transcendentals=0)
IN_ANY = pl.BlockSpec(memory_space=pl.ANY)
IN_VMEM = pl.BlockSpec(memory_space=pltpu.VMEM)


def stay(array):
    return pltpu.with_memory_space_constraint(array, pltpu.HBM)


def exchange(shard, axis, step):
    return lax.ppermute(shard, axis, [(i, i ^ step) for i in range(lax.axis_size(axis))])


def low_lanes(rows, width):
    return lax.broadcasted_iota(jnp.int32, (rows, width), 1) < width // 2


def split_halves(state):
    fields, width = state.shape[0] // 2, state.shape[1]
    real, imag = state[:fields], state[fields:]
    low = low_lanes(fields, width)
    first = jnp.where(low, real, pltpu.roll(imag, width // 2, 1))
    second = jnp.where(low, pltpu.roll(real, width // 2, 1), imag)
    return first.astype(jnp.bfloat16), second.astype(jnp.bfloat16)


def join_halves(first, second):
    fields, width = first.shape
    low = low_lanes(fields, width)
    first, second = first.astype(jnp.float32), second.astype(jnp.float32)
    real = jnp.where(low, first, pltpu.roll(second, width // 2, 1))
    imag = jnp.where(low, pltpu.roll(first, width // 2, 1), second)
    return jnp.concatenate([real, imag], 0).astype(jnp.bfloat16)


def dot(a, b):
    return jnp.dot(a, b, preferred_element_type=jnp.float32)


def upper_bit(level):
    return lax.axis_index("deg") >> level & 1


def put_halves(upper, state, own_ref, send_ref, g):
    first, second = split_halves(state)
    own_ref[g] = jnp.where(upper == 1, second, first)
    send_ref[g] = jnp.where(upper == 1, first, second)


def joined_state(upper, own_ref, came_ref, g):
    own, came = own_ref[g], came_ref[g]
    return join_halves(jnp.where(upper == 1, came, own), jnp.where(upper == 1, own, came))


def load_parts(source, target, sems):
    part = target.shape[0] // PARTS
    copies = []
    for n in range(PARTS):
        here = pl.ds(n * part, part)
        copies.append(pltpu.make_async_copy(source.at[here], target.at[here], sems.at[n]))
        copies[-1].start()
    return copies


def start_fetches(places, sources, targets, sems):
    copies = []
    for n, (place, source, target) in enumerate(zip(places, sources, targets)):
        copies.append(pltpu.make_async_copy(source.at[place], target, sems.at[n]))
        copies[-1].start()
    return copies


def leaf_kernel(places, *refs):
    fetches = len(places)
    coef, maps, skel, _, *sources = refs[: 4 + fetches]
    own_ref, send_ref, *targets = refs[4 + fetches : 6 + 2 * fetches]
    count, _, width = own_ref.shape
    degrees = maps.shape[1]
    scratch = refs[6 + 2 * fetches :]
    parts = []
    if len(scratch) > 3:
        coef_hbm, map_hbm, skel_hbm = coef, maps, skel
        coef, maps, skel, sems = scratch[:4]
        skel_copy = pltpu.make_async_copy(skel_hbm.at[pl.ds(0, count)], skel, sems.at[2, 0])
        skel_copy.start()
        parts = [load_parts(map_hbm, maps, sems.at[0]), load_parts(coef_hbm, coef, sems.at[1])]
    later = start_fetches(places, sources, targets, scratch[-1]) if fetches else []
    if parts:
        skel_copy.wait()
    rows = lax.broadcasted_iota(jnp.int32, (degrees, width), 0)
    for g in range(count):
        for copies in parts:
            if g % (count // PARTS) == 0:
                copies[g // (count // PARTS)].wait()
        picks = (rows == skel[g : g + 1, :]).astype(jnp.bfloat16)
        both = dot(coef[g], jnp.concatenate([maps[g], picks], 1))
        put_halves(upper_bit(0), both[:, :width] + both[:, width:], own_ref, send_ref, g)
    for copy in later:
        copy.wait()


def level_kernel(first, num, places, *refs):
    fetches = len(places)
    own_in, came_in, maps, _, *sources = refs[: 4 + fetches]
    own_ref, send_ref, *targets = refs[4 + fetches : 6 + 2 * fetches]
    later = start_fetches(places, sources, targets, refs[-1]) if fetches else []
    for g in range(own_in.shape[0]):
        joined = joined_state(upper_bit(num), own_in, came_in, g)
        put_halves(upper_bit(num + 1), dot(joined, maps[num, first + g]), own_ref, send_ref, g)
    for copy in later:
        copy.wait()


def last_kernel(first, num, offset, own_in, came_in, maps, lats, _, *refs):
    peers = lax.axis_size("wave")
    out_refs, (block_ref, moved_ref) = refs[-2 - peers : -2], refs[-2:]
    count, fields = own_in.shape[:2]
    share = fields // peers
    for g in range(count):
        joined = joined_state(upper_bit(num), own_in, came_in, g)
        node = dot(joined, maps[num, first + g]).astype(jnp.bfloat16)
        block_ref[g] = dot(node, lats[first + g]).astype(jnp.bfloat16)
    tile = 16
    size = tile * tile
    out_at = lax.broadcasted_iota(jnp.int32, (size, size), 0)
    in_at = lax.broadcasted_iota(jnp.int32, (size, size), 1)
    shift = tile.bit_length() - 1
    swap = (out_at >> shift) + ((out_at & tile - 1) << shift) == in_at
    swap = swap.astype(jnp.bfloat16)
    rows = block_ref.shape[2]
    me = lax.axis_index("wave")
    for g in range(0, count, tile):
        for c in range(0, 2 * fields, tile):
            moved = dot(swap, block_ref[g : g + tile, c : c + tile, :].reshape(size, rows)).astype(jnp.bfloat16)
            moved = moved.reshape(tile, tile, rows)
            part, field = c // fields, c % fields
            for at in range(0, tile, share):
                moved_ref[(field + at) // share, :, part, g : g + tile, :] = moved[at : at + share]
    for step, out_ref in enumerate(out_refs):
        out_ref[:, :, offset : offset + count, :] = moved_ref[me ^ step]


def table_kernel(lon_count, slots, sizes, first, count, map_ref, *refs):
    table_ref, q_ref = refs[-2:]
    me = lax.axis_index("wave")
    row = 0
    for n, size in enumerate(sizes):
        for step in range(map_ref.shape[0] // slots):
            start = (me ^ step) * slots + sum(sizes[:n])

            def put(m, carry, row=row, start=start):
                q_ref[pl.ds(row + m, 1), :] = jnp.full((1, LANES), map_ref[start + m], jnp.int32)
                return carry

            if first <= row < first + count:
                lax.fori_loop(0, size, put, 0, unroll=8)
            row += size
    scale = 2.0 * jnp.pi / lon_count
    lane = lax.broadcasted_iota(jnp.int32, (BLOCK, LANES), 1)

    def rows(i, carry):
        here = pl.ds(pl.multiple_of(i * BLOCK, BLOCK), BLOCK)
        q = q_ref[here, :]
        low = (q * lane & lon_count - 1).astype(jnp.float32) * scale
        high = (q * (lane * LANES) & lon_count - 1).astype(jnp.float32) * scale
        weight = jnp.where(q == 0, 1.0, 2.0).astype(jnp.float32)
        cl, sl = jnp.cos(low) * weight, jnp.sin(low) * -weight
        ch, sh = jnp.cos(high), jnp.sin(high)
        for h in range(table_ref.shape[2] // LANES):
            c, s = ch[:, h : h + 1], sh[:, h : h + 1]
            table_ref[0, here, h * LANES : (h + 1) * LANES] = (c * cl + s * sl).astype(jnp.bfloat16)
            table_ref[1, here, h * LANES : (h + 1) * LANES] = (c * sl - s * cl).astype(jnp.bfloat16)
        return carry

    lax.fori_loop(first // BLOCK, (first + count) // BLOCK, rows, 0)


def wave_table(wavemap, slots, sizes, lon_count, after, begun, first, count):
    total = wavemap.shape[0]
    return pl.pallas_call(
        functools.partial(table_kernel, lon_count, slots, sizes, first, count),
        in_specs=[pl.BlockSpec(memory_space=pltpu.SMEM), IN_ANY] + [IN_VMEM] * len(begun),
        input_output_aliases={2: 0} if begun else {},
        out_specs=IN_VMEM,
        out_shape=jax.ShapeDtypeStruct((2, total, lon_count // 2 + LANES), jnp.bfloat16),
        scratch_shapes=[pltpu.VMEM((total, LANES), jnp.int32)],
        cost_estimate=CHEAP,
        compiler_params=pltpu.CompilerParams(vmem_limit_bytes=16 * 2**20),
        name="table",
    )(wavemap, after, *begun)


def synthesis_kernel(*refs):
    block_refs = refs[:-6]
    table_ref, out_ref, left_ref, carry_ref, buffer_ref, sems = refs[-6:]
    fields, rows, lon_count = out_ref.shape
    slots, width = buffer_ref.shape[0], buffer_ref.shape[-1]
    for f in range(fields):
        for p in range(2):
            left_ref[p, f * rows : (f + 1) * rows, :] = jnp.concatenate([ref[f, p] for ref in block_refs], 0).T
    middle = pl.ds(lon_count // 2, LANES)
    carry_ref[...] = dot(left_ref[0], table_ref[0, :, middle]) - dot(left_ref[1], table_ref[1, :, middle])
    tiles = lon_count // width
    steps = tiles // 2
    size = ROWS
    lane = lax.broadcasted_iota(jnp.int32, (size, LANES), 1)
    mirror = (LANES - lane) % LANES

    def copies(i):
        slot, at = i % slots, steps - 1 - i
        straight = pl.ds(pl.multiple_of(at * width, width), width)
        turned = pl.ds(pl.multiple_of((tiles - 1 - at) * width, width), width)
        return (
            pltpu.make_async_copy(buffer_ref.at[slot, 0], out_ref.at[:, :, straight], sems.at[slot, 0]),
            pltpu.make_async_copy(buffer_ref.at[slot, 1], out_ref.at[:, :, turned], sems.at[slot, 1]),
        )

    def step(i, carry):
        slot, at = i % slots, steps - 1 - i
        straight = pl.ds(pl.multiple_of(at * width, width), width)

        @pl.when(i >= slots)
        def _():
            for copy in copies(i - slots):
                copy.wait()

        for r in range(0, fields * rows, size):
            f = r // rows
            n = size // rows
            cos_sum = dot(left_ref[0, r : r + size, :], table_ref[0, :, straight])
            sin_sum = dot(left_ref[1, r : r + size, :], table_ref[1, :, straight])
            buffer_ref[slot, 0, f : f + n] = (cos_sum + sin_sum).astype(jnp.bfloat16).reshape(n, rows, width)
            back = cos_sum - sin_sum
            following = carry_ref[r : r + size, :]
            for t in reversed(range(width // LANES)):
                piece = back[:, t * LANES : (t + 1) * LANES]
                turned = jnp.take_along_axis(piece, mirror, axis=1, mode="promise_in_bounds")
                turned = jnp.where(lane == 0, following, turned).astype(jnp.bfloat16)
                to = width - (t + 1) * LANES
                buffer_ref[slot, 1, f : f + n, :, to : to + LANES] = turned.reshape(n, rows, LANES)
                following = piece
            carry_ref[r : r + size, :] = following
        for copy in copies(i):
            copy.start()
        return carry

    lax.fori_loop(0, steps, step, 0, unroll=UNROLL)
    for i in range(max(0, steps - slots), steps):
        for copy in copies(i):
            copy.wait()


def synthesis(blocks, table, lon_count):
    fields, _, _, rows = blocks[0].shape
    depth = table.shape[1]
    return pl.pallas_call(
        synthesis_kernel,
        in_specs=[IN_VMEM] * (len(blocks) + 1),
        out_specs=pl.BlockSpec(memory_space=pl.ANY),
        out_shape=jax.ShapeDtypeStruct((fields, rows, lon_count), jnp.bfloat16),
        scratch_shapes=[
            pltpu.VMEM((2, fields * rows, depth), jnp.bfloat16),
            pltpu.VMEM((fields * rows, LANES), jnp.float32),
            pltpu.VMEM((SLOTS, 2, fields, rows, TILE), jnp.bfloat16),
            pltpu.SemaphoreType.DMA((SLOTS, 2)),
        ],
        cost_estimate=CHEAP,
        compiler_params=pltpu.CompilerParams(vmem_limit_bytes=32 * 2**20),
        name="synthesis",
    )(*blocks, table)


def body(spectrum, leaf_map, level_maps, lat_map, skeleton, wavemap):
    slots, _, fields, degrees = spectrum.shape
    columns = 2 * fields
    width = leaf_map.shape[2]
    levels = level_maps.shape[0]
    rows = lat_map.shape[2]
    coef = spectrum.reshape(slots, columns, degrees)
    peers = lax.axis_size("wave")
    sizes = [slots * share // sum(SHARES) for share in SHARES]
    firsts = [sum(sizes[:n]) for n in range(len(sizes))]
    chunks = range(len(sizes))
    params = pltpu.CompilerParams(vmem_limit_bytes=16 * 2**20)

    def half(chunk):
        return jax.ShapeDtypeStruct((sizes[chunk], fields, width), jnp.bfloat16)

    def fetched(fetches):
        shapes = []
        for array, place in fetches:
            view = jax.eval_shape(lambda a, place=place: a[place], array)
            shapes.append(jax.ShapeDtypeStruct(view.shape, view.dtype))
        sems = [pltpu.SemaphoreType.DMA((len(fetches),))] if fetches else []
        return [stay(array) for array, _ in fetches], [at(place) for _, place in fetches], shapes, sems

    def at(place):
        return pl.ds(place.start, place.stop - place.start) if isinstance(place, slice) else place

    def leaf(chunk, inputs, after, fetches):
        count = sizes[chunk]
        sources, places, shapes, sems = fetched(fetches)
        scratch = [] if chunk else [
            pltpu.VMEM((count, columns, degrees), jnp.bfloat16),
            pltpu.VMEM((count, degrees, width), jnp.bfloat16),
            pltpu.VMEM((count, width), jnp.int32),
            pltpu.SemaphoreType.DMA((3, PARTS)),
        ]
        return pl.pallas_call(
            functools.partial(leaf_kernel, places),
            in_specs=[IN_VMEM if chunk else IN_ANY] * 3 + [IN_ANY] * (1 + len(fetches)),
            out_specs=[IN_VMEM] * (2 + len(fetches)),
            out_shape=[half(chunk)] * 2 + shapes,
            scratch_shapes=scratch + sems,
            cost_estimate=CHEAP,
            compiler_params=params,
            name="leaf",
        )(*inputs, after, *sources)

    def level(chunk, num, own, came, maps, after, fetches):
        count = sizes[chunk]
        sources, places, shapes, sems = fetched(fetches)
        return pl.pallas_call(
            functools.partial(level_kernel, firsts[chunk], num, places),
            in_specs=[IN_VMEM] * 3 + [IN_ANY] * (1 + len(fetches)),
            out_specs=[IN_VMEM] * (2 + len(fetches)),
            out_shape=[half(chunk)] * 2 + shapes,
            scratch_shapes=sems,
            cost_estimate=CHEAP,
            compiler_params=params,
            name="level",
        )(own, came, maps, after, *sources)

    def last(chunk, own, came, maps, lats, after, group, begun):
        count = sizes[chunk]
        piece = jax.ShapeDtypeStruct((fields // peers, 2, sum(sizes[n] for n in group), rows), jnp.bfloat16)
        return pl.pallas_call(
            functools.partial(last_kernel, firsts[chunk], levels - 1, firsts[chunk] - firsts[group[0]]),
            in_specs=[IN_VMEM] * 4 + [IN_ANY] + [IN_VMEM] * len(begun),
            out_specs=[IN_VMEM] * peers,
            out_shape=[piece] * peers,
            input_output_aliases={5 + n: n for n in range(len(begun))},
            scratch_shapes=[
                pltpu.VMEM((count, columns, rows), jnp.bfloat16),
                pltpu.VMEM((peers, fields // peers, 2, count, rows), jnp.bfloat16),
            ],
            cost_estimate=CHEAP,
            compiler_params=params,
            name="last",
        )(own, came, maps, lats, after, *begun)

    whole = [coef, leaf_map, skeleton]
    order = [(chunk, stage) for chunk in chunks for stage in range(levels + 1)]
    order.sort(key=lambda turn: (sum(turn), TURN * turn[0]))
    wanted = []
    for chunk, stage in order:
        if stage == 0 and chunk:
            ahead = slice(firsts[chunk], firsts[chunk] + sizes[chunk])
            wanted.append((("leaf", chunk), [(array, ahead) for array in whole]))
    wanted.reverse()
    held = {("leaf", 0): [stay(array) for array in whole]}
    before, table, filled = stay(skeleton), None, 0
    group_sizes = [sum(sizes[n] for n in group) for group in GROUPS]
    share_rows = slots * peers // (1 + len(TABLE_AT))

    def make_table(after, table):
        nonlocal filled
        begun = [] if table is None else [table]
        filled += share_rows
        return wave_table(wavemap, slots, group_sizes, NLON, after, begun, filled - share_rows, share_rows)

    state, begun, blocks = {}, [], []
    for chunk, stage in order:
        name, fetches = wanted.pop() if wanted and stage == 0 else (None, [])
        if (chunk, stage) in TABLE_AT:
            before = table = make_table(before, table)
        if stage == levels:
            group = next(group for group in GROUPS if chunk in group)
            begun = last(chunk, *state[chunk], level_maps, lat_map, before, group, begun)
            before = begun[0]
            if chunk == group[-1]:
                blocks += [p if step == 0 else exchange(p, "wave", step) for step, p in enumerate(begun)]
                begun = []
            continue
        if stage == 0:
            before, send, *more = leaf(chunk, held["leaf", chunk], before, fetches)
        else:
            before, send, *more = level(chunk, stage - 1, *state[chunk], level_maps, before, fetches)
        held[name] = more
        state[chunk] = before, exchange(send, "deg", 1 << stage)
    while filled < slots * peers:
        before = table = make_table(before, table)
    return synthesis(blocks, table, NLON)


def solution(mesh):
    placed = (
        P("wave", None, None, "deg"),
        P("wave", "deg", None),
        P(None, "wave", "deg", None),
        P("wave", None, "deg"),
        P("wave", "deg"),
        P(),
    )
    return jax.shard_map(
        body, mesh=mesh, in_specs=placed, out_specs=P("wave", "deg", None), check_vma=False
    )
```
